512 devices in a mesh: space: 32 (over x, y), bins: 16 (over z, core).
Axes of the slice: x: 4, y: 8, z: 8, core: 2. Of those that a mesh axis runs over, the one named last changes fastest.
Arguments:
- swell_density_ensemble: bfloat16 [768, 32, 8192], P('bins', None, 'space'), may hold values from 0.049804688 to 2
- neighbors: int32 [4, 8192], P(None, 'space'), may hold values from -1 to 8191, as said below
- obs_operator: float32 [16, 768], P(None, 'bins'), may hold values from -0.21875 to 0.21875
- obs_point: int32 [2048], P('space'), may hold values from 0 to 8191, as said below
- obs_type: int32 [2048], P('space'), may hold values from 0 to 15
- obs_value: float32 [2048], P('space'), may hold values from -8 to 8
- obs_var: float32 [2048], P('space'), may hold values from 0.05 to 0.5
- obs_list: int32 [32, 8192], P(None, 'space'), may hold values from -1 to 2047, as said below
- obs_count: int32 [8192], P('space'), may hold values from 0 to 32, as said below
Outputs:
- analysis: bfloat16 [768, 32, 8192], P('bins', None, 'space')
The draws below stay inside these ranges and needn't reach their ends.
Inputs may be any that keep to these rules, and one draw needn't show every extreme that they name: `neighbors`: row k of point p holds p - 32, p + 32, p - 1 or p + 1 for k = 0, 1, 2, 3, the last two only within p's column, or -1 where that neighbour is land or off the grid. `obs_point`: observation j lies on a point of tile j // 64, where tile t holds points t * 256 to (t + 1) * 256 - 1. `obs_list`: for k < obs_count[p], slot k of point p names an observation whose point lies within 6 cells of p (squared column offset plus squared row offset at most 6^2), so in p's tile or a tile beside it; names in one list are distinct; other slots hold -1. `obs_count`: reaches 32 at some point of every tile.
All inputs are finite; a program needn't handle non-finite values.
Results may differ from the reference program's by a relative error of at most 0.0059.
Values may be sent and summed in bfloat16 or wider, within the bound.
A program may use at most 64 MiB of HBM per device.

```python
import math
import jax
import jax.numpy as jnp
from jax import lax

ND = 24
MEMBERS = 32
ROWS = 32
COLS_DEV = 8
OBS_LIST = 32
LOC_R = 6
NTYPE = 16
NS_ITERS = 8
FREQ_DIR_CELLS = 768
PATCH_WET_SITES = 256
OBS_TILE = 64
POINTS = 8192
NOBS = 2048


def obs_layout(key):
    tile_count = POINTS // PATCH_WET_SITES
    half_obs = OBS_TILE // 2
    corner_col = jax.random.randint(jax.random.fold_in(key, 101), (tile_count, 1), 0, COLS_DEV - 3)
    corner_row = jax.random.randint(jax.random.fold_in(key, 102), (tile_count, 1), 0, ROWS - 7)
    near_col = corner_col + jax.random.randint(jax.random.fold_in(key, 103), (tile_count, half_obs), 0, 4)
    near_row = corner_row + jax.random.randint(jax.random.fold_in(key, 104), (tile_count, half_obs), 0, 8)
    far_col = jax.random.randint(jax.random.fold_in(key, 105), (tile_count, OBS_TILE - half_obs), 0, COLS_DEV)
    far_row = jax.random.randint(jax.random.fold_in(key, 106), (tile_count, OBS_TILE - half_obs), 0, ROWS)
    local_col = jnp.concatenate([near_col, far_col], axis=1)
    local_row = jnp.concatenate([near_row, far_row], axis=1)
    tile_ids = jnp.arange(tile_count, dtype=jnp.int32)[:, None]
    obs_points = ((tile_ids * COLS_DEV + local_col) * ROWS + local_row).astype(jnp.int32)
    cand_tile = tile_ids + jnp.array([-1, 0, 1], dtype=jnp.int32)[None]
    valid_tile = (cand_tile >= 0) & (cand_tile < tile_count)
    clipped = jnp.clip(cand_tile, 0, tile_count - 1)
    cand_points = obs_points[clipped].reshape(tile_count, 3 * OBS_TILE)
    cand_ids = (clipped[:, :, None] * OBS_TILE + jnp.arange(OBS_TILE, dtype=jnp.int32)[None, None]).reshape(tile_count, 3 * OBS_TILE)
    cand_valid = jnp.repeat(valid_tile, OBS_TILE, axis=1)
    point_ids = tile_ids * PATCH_WET_SITES + jnp.arange(PATCH_WET_SITES, dtype=jnp.int32)[None]
    col_gap = cand_points[:, None, :] // ROWS - point_ids[:, :, None] // ROWS
    row_gap = cand_points[:, None, :] % ROWS - point_ids[:, :, None] % ROWS
    within = (col_gap * col_gap + row_gap * row_gap <= LOC_R * LOC_R) & cand_valid[:, None, :]
    jitter = jax.random.randint(jax.random.fold_in(key, 107), (tile_count, PATCH_WET_SITES, 3 * OBS_TILE), 0, 4096)
    ranking = within.astype(jnp.int32) * 2 ** 24 + jitter * 2048 + jnp.arange(3 * OBS_TILE, dtype=jnp.int32)[None, None]
    top_scores, top_index = lax.top_k(ranking, OBS_LIST)
    within_count = jnp.sum(within.astype(jnp.int32), axis=2)
    cap = jax.random.randint(jax.random.fold_in(key, 108), (tile_count, PATCH_WET_SITES), OBS_LIST // 4, OBS_LIST + 1)
    fullest = jnp.argmax(within_count, axis=1).astype(jnp.int32)
    cap = jnp.where(jnp.arange(PATCH_WET_SITES, dtype=jnp.int32)[None] == fullest[:, None], OBS_LIST, cap)
    counts = jnp.minimum(jnp.minimum(within_count, cap), OBS_LIST).astype(jnp.int32)
    spread_ids = jnp.broadcast_to(cand_ids[:, None, :], (tile_count, PATCH_WET_SITES, 3 * OBS_TILE))
    chosen = jnp.take_along_axis(spread_ids, top_index, axis=2)
    slot_live = jnp.arange(OBS_LIST, dtype=jnp.int32)[None, None] < counts[:, :, None]
    lists = jnp.where(slot_live, chosen, -1).astype(jnp.int32)
    return (obs_points.reshape(NOBS), jnp.transpose(lists.reshape(POINTS, OBS_LIST)), counts.reshape(POINTS))


def draw_obs_point(key, part):
    return obs_layout(key)[0]


def draw_obs_list(key, part):
    return obs_layout(key)[1]


def draw_obs_count(key, part):
    return obs_layout(key)[2]


def draw_neighbors(key, part):
    point_ids = jnp.arange(POINTS, dtype=jnp.int32)
    row_index = point_ids % ROWS
    col_index = point_ids // ROWS
    col_total = POINTS // ROWS
    offsets = jnp.array([-ROWS, ROWS, -1, 1], dtype=jnp.int32)[:, None]
    inside = jnp.stack([col_index > 0, col_index < col_total - 1, row_index > 0, row_index < ROWS - 1])
    coast = jax.random.randint(jax.random.fold_in(key, 5), (4, POINTS), 0, 100) < 15
    return jnp.where(inside & jnp.logical_not(coast), point_ids[None] + offsets, -1).astype(jnp.int32)


def place_ends(entries, rng, smallest, high):
    longest = entries.shape.index(max(entries.shape))
    spots = []
    for shift in (0, 1):
        where = [jax.random.randint(jax.random.fold_in(rng, axis), (), 0, length) for axis, length in enumerate(entries.shape)]
        where[longest] = (where[longest] + shift) % entries.shape[longest]
        spots.append(tuple(where))
    return entries.at[spots[0]].set(smallest).at[spots[1]].set(high)


def steps_of(key, extent, pieces, smallest, top_value):
    loudness, own = 1.0, jax.random.fold_in(key, 6)
    for axis_at, blocks in pieces:
        steps = jnp.exp(jax.random.uniform(jax.random.fold_in(own, axis_at), (blocks,), jnp.float32, smallest / len(pieces), top_value / len(pieces)))
        loudness = loudness * jnp.repeat(steps, extent[axis_at] // blocks).reshape([-1 if axis == axis_at else 1 for axis in range(len(extent))])
    return loudness


def gaussian(key, dims, scale, bound, split=(), kind=jnp.bfloat16):
    entries = jax.random.normal(key, dims, jnp.float32) * scale
    if len(split) > 0:
        entries = steps_of(key, dims, split, -0.22, 0.18) * entries
    return jnp.clip(entries, min=-bound, max=bound).astype(kind)


def setup_inputs(seed: int = 0) -> dict:
    streams_of = jax.random.split(jax.random.key(seed), 10)
    return {
        "swell_density_ensemble": jnp.clip(jnp.exp(math.log(2.0) - 3.6927934 * jax.random.uniform(streams_of[0], (FREQ_DIR_CELLS, MEMBERS, POINTS), jnp.float32) ** steps_of(streams_of[0], (FREQ_DIR_CELLS, MEMBERS, POINTS), ((0, 16), (2, 32)), -0.2, 0.2)), 0.049804688, 2.0).astype(jnp.bfloat16),
        "neighbors": draw_neighbors(jax.random.fold_in(streams_of[9], 71), 0),
        "obs_operator": gaussian(streams_of[2], (NTYPE, FREQ_DIR_CELLS), FREQ_DIR_CELLS ** -0.5, 0.21875, ((1, 16),), jnp.float32),
        "obs_point": draw_obs_point(jax.random.fold_in(streams_of[9], 71), 0),
        "obs_type": place_ends(jax.random.randint(streams_of[4], (NOBS,), 0, NTYPE), jax.random.fold_in(streams_of[4], 1), 0, NTYPE - 1).astype(jnp.int32),
        "obs_value": gaussian(streams_of[5], (NOBS,), 1.5, 8.0, ((0, 32),), jnp.float32),
        "obs_var": jnp.clip(jnp.exp(math.log(0.5) - 2.3025851 * jax.random.uniform(streams_of[6], (NOBS,), jnp.float32) ** steps_of(streams_of[6], (NOBS,), ((0, 32),), -0.2, 0.2)), 0.05, 0.5),
        "obs_list": draw_obs_list(jax.random.fold_in(streams_of[9], 71), 0),
        "obs_count": draw_obs_count(jax.random.fold_in(streams_of[9], 71), 0),
    }


courant_max = 0.7
freq_ratio = 1.1

def courant(frequency_direction_number):
    direction = (frequency_direction_number % ND).astype(jnp.float32)
    band_index = (frequency_direction_number // ND).astype(jnp.float32)
    angle = 2.0 * jnp.pi * (direction + 0.5) / ND
    speed = courant_max * jnp.exp(-band_index * jnp.log(freq_ratio))
    cosine = jnp.cos(angle)
    sine_value = jnp.sin(angle)
    return ((speed * jnp.abs(cosine))[:, None, None], (speed * jnp.abs(sine_value))[:, None, None], (cosine > 0)[:, None, None], (sine_value > 0)[:, None, None])

def donor_cell_propagate(padded_with_neighbours, outer_edge_inflow, frequency_direction_number):
    inner = padded_with_neighbours.shape[2] - 2 * ROWS
    swell_variance_density = padded_with_neighbours[:, :, ROWS:ROWS + inner].astype(jnp.float32)
    from_west = padded_with_neighbours[:, :, 0:inner].astype(jnp.float32) * outer_edge_inflow[0]
    from_east = padded_with_neighbours[:, :, 2 * ROWS:2 * ROWS + inner].astype(jnp.float32) * outer_edge_inflow[1]
    from_south = padded_with_neighbours[:, :, ROWS - 1:ROWS - 1 + inner].astype(jnp.float32) * outer_edge_inflow[2]
    from_north = padded_with_neighbours[:, :, ROWS + 1:ROWS + 1 + inner].astype(jnp.float32) * outer_edge_inflow[3]
    courant_x, courant_y, east_ward, north_ward = courant(frequency_direction_number)
    inflow_x = jnp.where(east_ward, from_west, from_east)
    inflow_y = jnp.where(north_ward, from_south, from_north)
    return (swell_variance_density - courant_x * (swell_variance_density - inflow_x) - courant_y * (swell_variance_density - inflow_y)).astype(jnp.bfloat16)

def obs_package(predicted, obs_point, obs_value, obs_var):
    ens_mean = lax.optimization_barrier(jnp.mean(predicted, axis=0))
    weight = lax.rsqrt(obs_var)
    anomaly = (predicted - ens_mean[None]) * weight[None]
    innovation = (obs_value - ens_mean) * weight
    obs_col = (obs_point // ROWS).astype(jnp.float32)
    obs_row = (obs_point % ROWS).astype(jnp.float32)
    return jnp.concatenate([anomaly, innovation[None], obs_col[None], obs_row[None]], axis=0)

def analysis_weights(anomaly, innovation, taper):
    members = anomaly.shape[0]
    highest = lax.Precision.HIGHEST
    identity = jnp.eye(members, dtype=jnp.float32)[None]
    weighted = anomaly * taper[None]
    matrix = identity + jnp.einsum('ikn,jkn->nij', weighted, anomaly, precision=highest) / (members - 1.0)
    obs_pull = jnp.einsum('ikn,kn->ni', weighted, innovation, precision=highest) / (members - 1.0)
    scale = jnp.sqrt(lax.optimization_barrier(jnp.sum(matrix * matrix, axis=(1, 2))))
    current = matrix / scale[:, None, None]
    inverse = jnp.broadcast_to(identity, matrix.shape).astype(jnp.float32)

    def newton_step(iteration, carried):
        current, inverse = carried
        factor = 1.5 * identity - 0.5 * jnp.einsum('nij,njk->nik', inverse, current, precision=highest)
        current = jnp.einsum('nij,njk->nik', current, factor, precision=highest)
        inverse = jnp.einsum('nij,njk->nik', factor, inverse, precision=highest)
        return (current, inverse)
    current, inverse = lax.fori_loop(0, NS_ITERS, newton_step, (current, inverse))
    inv_root = inverse / jnp.sqrt(scale)[:, None, None]
    half_step = jnp.einsum('nij,nj->ni', inv_root, obs_pull, precision=highest)
    mean_shift = jnp.einsum('nij,nj->ni', inv_root, half_step, precision=highest)
    return jnp.transpose(inv_root + mean_shift[:, :, None], (1, 2, 0))

def point_weights(package, slot_ids, counts, first_point):
    members = package.shape[0] - 3
    safe_slots = jnp.maximum(slot_ids, 0)
    picked = jnp.take(package, safe_slots, axis=1)
    points = first_point + jnp.arange(slot_ids.shape[1], dtype=jnp.int32)
    point_col = (points // ROWS).astype(jnp.float32)
    point_row = (points % ROWS).astype(jnp.float32)
    active = (jnp.arange(slot_ids.shape[0], dtype=jnp.int32)[:, None] < counts[None]).astype(jnp.float32)
    distance = (picked[members + 1] - point_col[None]) ** 2 + (picked[members + 2] - point_row[None]) ** 2
    taper = (1.0 - distance / (2.0 * LOC_R * LOC_R)) ** 2 * active
    return analysis_weights(picked[:members], picked[members], taper)

def combine_ensemble_coefficients(prior_ensemble_densities, ensemble_mixing_coefficients):
    swell_variance_density = prior_ensemble_densities.astype(jnp.float32)
    ens_mean = lax.optimization_barrier(jnp.mean(swell_variance_density, axis=1, keepdims=True))
    anomaly = swell_variance_density - ens_mean
    moved = jnp.einsum('bin,imn->bmn', anomaly, ensemble_mixing_coefficients, precision=lax.Precision.HIGHEST)
    return (ens_mean + moved).astype(jnp.bfloat16)

def reference(swell_density_ensemble, neighbors, obs_operator, obs_point, obs_type, obs_value, obs_var, obs_list, obs_count):
    outer_edge_inflow = (neighbors >= 0).astype(jnp.float32)

    def lone_frequency_direction(items):
        swell_variance_density, bin_index = items
        padded_with_neighbours = jnp.pad(swell_variance_density[None], ((0, 0), (0, 0), (ROWS, ROWS)))
        return donor_cell_propagate(padded_with_neighbours, outer_edge_inflow, bin_index[None])[0]
    prior_ensemble_densities = lax.map(lone_frequency_direction, (swell_density_ensemble, jnp.arange(FREQ_DIR_CELLS, dtype=jnp.int32)))
    tile_count = POINTS // PATCH_WET_SITES

    def tile_terms(items):
        measured_locations, obs_kinds = items
        lattice_width_count = jnp.take(prior_ensemble_densities, measured_locations, axis=2).astype(jnp.float32)
        obs_rows = obs_operator[obs_kinds]
        return jnp.einsum('bmo,ob->mo', lattice_width_count, obs_rows, precision=lax.Precision.HIGHEST)
    predicted = lax.map(tile_terms, (obs_point.reshape(tile_count, OBS_TILE), obs_type.reshape(tile_count, OBS_TILE)))
    predicted = jnp.transpose(predicted, (1, 0, 2)).reshape(MEMBERS, NOBS)
    package = obs_package(predicted, obs_point, obs_value, obs_var)
    slot_tiles = jnp.transpose(obs_list.reshape(OBS_LIST, tile_count, PATCH_WET_SITES), (1, 0, 2))
    count_tiles = obs_count.reshape(tile_count, PATCH_WET_SITES)
    package_wide = jnp.pad(package, ((0, 0), (OBS_TILE, OBS_TILE)))

    def tile_analysis(items):
        slot_ids, counts, present_patch_number = items
        offset = (present_patch_number - 1) * OBS_TILE
        local_slots = jnp.where(slot_ids >= 0, slot_ids - offset, -1)
        obs_wide = lax.dynamic_slice_in_dim(package_wide, present_patch_number * OBS_TILE, 3 * OBS_TILE, 1)
        ensemble_mixing_coefficients = point_weights(obs_wide, local_slots, counts, present_patch_number * PATCH_WET_SITES)
        patch_ocean_subarray = lax.dynamic_slice_in_dim(prior_ensemble_densities, present_patch_number * PATCH_WET_SITES, PATCH_WET_SITES, 2)
        return combine_ensemble_coefficients(patch_ocean_subarray, ensemble_mixing_coefficients)
    result = lax.map(tile_analysis, (slot_tiles, count_tiles, jnp.arange(tile_count, dtype=jnp.int32)))
    return jnp.transpose(result, (1, 2, 0, 3)).reshape(FREQ_DIR_CELLS, MEMBERS, POINTS)
```

```python
import functools
import math

import jax
import jax.numpy as jnp
import numpy as np
from jax import lax
from jax.experimental import pallas as pl
from jax.experimental.pallas import tpu as pltpu
from jax.sharding import PartitionSpec as P

ND = 24
ROWS = 32
LOC_R = 6
NS_ITERS = 8
COURANT_MAX = 0.7
FREQ_RATIO = 1.1

BINS = 48
MEM = 32
PTS = 256
OBS = 64
NEAR = 3 * OBS
OWN = 16
GROUPS = 2 * OWN
TILES = 32
ZC = 8
SIX = 6
WEST = ((0, 0), (0, 3), (1, 0), (1, 3))
EAST = ((0, 1), (0, 2), (1, 1), (1, 2))

MESH = pl.DeviceIdType.MESH
F32 = jnp.float32
BF16 = jnp.bfloat16


def iota(shape, dim):
    return lax.broadcasted_iota(jnp.int32, shape, dim)


def dot(a, b):
    return jnp.dot(a, b, preferred_element_type=F32)


def split(a):
    high = a.astype(BF16)
    return high, (a - high.astype(F32)).astype(BF16)


def stacked(a):
    return jnp.concatenate(split(a), axis=0)


def folded(a):
    half = a.shape[0] // 2
    return a[:half] + a[half:]


def block_diagonal(rows, mask):
    return jnp.concatenate([rows.astype(BF16)] * 8, axis=0) * mask


def lanes_roll(a, by):
    return pltpu.roll(a, by % 128, 1)


def exchange_kernel(
    cos_ref, sin_ref, x_ref, nb_ref, opw_ref, opt_ref, oty_ref, oval_ref, ovar_ref, olist_ref, ocnt_ref,
    l_ref, t_ref,
    a1, a2, a3, send_w, send_e, recv_w, recv_e, meta, meta_l, meta_r, fore, sums, core_in, chip_sum, z_in,
    total, total_l, total_r, relay, w8, expand, m_s, z_s, g_s, ssem, rsem,
):
    tile = lax.axis_index("space")
    me = lax.axis_index("bins")
    core = me % 2
    left, right = (tile + TILES - 1) % TILES, (tile + 1) % TILES
    mate = me + 1 - 2 * core

    barrier = pltpu.get_barrier_semaphore()
    partners = [(left, me), (right, me), (tile, mate)]
    partners += [(tile, (me + 2 * k) % (2 * ZC)) for k in (4, 3, 5, 2, 6, 1, 7)]
    for who in partners:
        pl.semaphore_signal(barrier, inc=1, device_id=who, device_id_type=MESH)

    def copy(src, dst, n, who):
        return pltpu.make_async_remote_copy(
            src_ref=src, dst_ref=dst, send_sem=ssem.at[n], recv_sem=rsem.at[n], device_id=who, device_id_type=MESH
        )

    lane = iota((MEM, 128), 1)
    block = lane // 32

    def pack(j, _):
        for bins, buf, half, at in ((WEST, send_w, 1, 96), (EAST, send_e, 0, 0)):
            out = None
            for k, (f, q) in enumerate(bins):
                edge = x_ref[f * ND + q * SIX + j, :, 128 * half : 128 * half + 128].astype(F32)
                edge = lanes_roll(edge, 32 * k - at)
                out = edge if out is None else jnp.where(block == k, edge, out)
            buf[j] = out.astype(BF16)
        return 0

    lax.fori_loop(0, SIX, pack, 0)

    zeros = jnp.zeros((1, OBS), F32)
    point = opt_ref[...]
    rows = [
        (point // ROWS).astype(F32), (point % ROWS).astype(F32), oval_ref[...], lax.rsqrt(ovar_ref[...]),
        zeros, zeros, zeros, zeros,
    ]
    packed = jnp.concatenate(rows, axis=0)
    meta[...] = jnp.concatenate([packed, jnp.zeros((8, OBS), F32)], axis=1)

    freq = (jnp.where(iota((BINS, PTS), 0) >= ND, 1, 0) + 2 * me).astype(F32)
    speed = COURANT_MAX * jnp.exp(-freq * math.log(FREQ_RATIO))
    open_side = (nb_ref[...] >= 0).astype(F32)
    cosine, sine = cos_ref[...], sin_ref[...]
    cx, cy = speed * jnp.abs(cosine), speed * jnp.abs(sine)
    a1[...] = 1.0 - cx - cy
    a2[...] = cx * jnp.where(cosine > 0, open_side[0:1], open_side[1:2])
    a3[...] = cy * jnp.where(sine > 0, open_side[2:3], open_side[3:4])

    here = (iota((PTS, OBS), 0) == point - tile * PTS).astype(BF16)
    kinds = (iota((16, OBS), 0) == oty_ref[...]).astype(F32)
    weights = lax.dot_general(
        opw_ref[...], kinds, (((0,), (0,)), ((), ())), precision=lax.Precision.HIGHEST, preferred_element_type=F32
    )

    pl.semaphore_wait(barrier, len(partners))
    halo = [
        copy(send_w, recv_w, 0, (right, me)),
        copy(send_e, recv_e, 1, (left, me)),
        copy(meta, meta_l, 2, (right, me)),
        copy(meta, meta_r, 3, (left, me)),
    ]
    for c in halo:
        c.start()

    ids = jnp.where(iota((MEM, PTS), 0) < ocnt_ref[...], olist_ref[...] - (tile - 1) * OBS, -1)
    ids = jnp.where(olist_ref[...] >= 0, ids, -1)
    low, high = ids[:, :128], ids[:, 128:]
    low = jnp.where(core == 0, low, lanes_roll(low, -32))
    high = jnp.where(core == 0, high, lanes_roll(high, -32))
    ids = jnp.where(
        block == 0, low, jnp.where(block == 1, lanes_roll(low, -32), jnp.where(block == 2, lanes_roll(high, 64), lanes_roll(high, 32)))
    )
    number = iota((NEAR, 128), 0)
    used = jnp.zeros((NEAR, 128), F32)
    for slot in range(MEM):
        used = jnp.where(ids[slot : slot + 1] == number, 1.0, used)

    for c in halo:
        c.wait_recv()

    def propagate(j, _):
        w_in = recv_w[j].astype(F32)
        e_in = recv_e[j].astype(F32)
        for f in range(2):
            for q in range(4):
                b = f * ND + q * SIX + j
                xl = x_ref[b, :, 0:128].astype(F32)
                xr = x_ref[b, :, 128:256].astype(F32)
                if (f, q) in WEST:
                    edge = lanes_roll(w_in, -32 * WEST.index((f, q)))
                    near, far = lanes_roll(xl, 32), lanes_roll(xr, 32)
                    ixl = jnp.where(block == 0, edge, near)
                    ixr = jnp.where(block == 0, near, far)
                else:
                    edge = lanes_roll(e_in, 96 - 32 * EAST.index((f, q)))
                    near, far = lanes_roll(xl, 96), lanes_roll(xr, 96)
                    ixl = jnp.where(block == 3, far, near)
                    ixr = jnp.where(block == 3, edge, far)
                turn = 1 if q < 2 else 127
                iyl, iyr = lanes_roll(xl, turn), lanes_roll(xr, turn)
                r1, r2, r3 = a1[pl.ds(b, 1), :], a2[pl.ds(b, 1), :], a3[pl.ds(b, 1), :]
                fore[b, :, 0:128] = (xl * r1[:, :128] + ixl * r2[:, :128] + iyl * r3[:, :128]).astype(BF16)
                fore[b, :, 128:256] = (xr * r1[:, 128:] + ixr * r2[:, 128:] + iyr * r3[:, 128:]).astype(BF16)
        return 0

    lax.fori_loop(0, SIX, propagate, 0)

    predicted = jnp.zeros((MEM, OBS), F32)
    for part in range(4):
        at = dot(fore[12 * part : 12 * part + 12].reshape(12 * MEM, PTS), here)
        for i in range(12):
            b = 12 * part + i
            predicted += at[MEM * i : MEM * (i + 1)] * weights[b : b + 1]
    sums[...] = jnp.concatenate([predicted[:16], predicted[16:]], axis=1)
    pair = copy(sums, core_in, 4, (tile, mate))
    pair.start()

    metas = jnp.concatenate(
        [
            jnp.where(iota((8, 128), 1) < OBS, meta_l[...], lanes_roll(meta[...], 64)),
            jnp.where(iota((8, 128), 1) < OBS, meta_r[...], 0.0),
        ],
        axis=1,
    )
    places = jnp.concatenate([metas, jnp.zeros((120, PTS), F32)], axis=0).T
    own_lane = iota((NEAR, 128), 1)
    col = (tile * 8 + 2 * (own_lane // 32) + core).astype(F32)
    row = (own_lane % 32).astype(F32)
    distance = (places[:NEAR, 0:1] - col) ** 2 + (places[:NEAR, 1:2] - row) ** 2
    taper = (1.0 - distance / (2.0 * LOC_R * LOC_R)) ** 2 * used
    taper_high, taper_low = split(taper)

    pair.wait_recv()
    chip_sum[...] = sums[...] + core_in[...]
    far = [copy(chip_sum, z_in.at[k - 1], 4 + k, (tile, (me + 2 * k) % (2 * ZC))) for k in (4, 3, 5, 2, 6, 1, 7)]
    for c in far:
        c.start()

    big_lane = iota((128, PTS), 1)
    target = 32 * ((big_lane // 32) % 4) + big_lane // 128
    source = iota((128, PTS), 0)
    for g in range(OWN):
        spread = (source == target + 2 * g).astype(BF16)
        expand[g] = spread
        w8[g] = dot(taper_high, spread).astype(BF16)

    def turn_in(i, _):
        f0, f1 = fore[2 * i].astype(F32), fore[2 * i + 1].astype(F32)
        parts = []
        for q in range(4):
            h = q // 2
            c0, c1 = f0[:, 128 * h : 128 * h + 128], f1[:, 128 * h : 128 * h + 128]
            if q % 2 == 0:
                parts.append(jnp.where(lane < 64, c0, lanes_roll(c1, 64)))
            else:
                parts.append(jnp.where(lane < 64, lanes_roll(c0, 64), c1))
        turned = jnp.concatenate(parts, axis=0).T
        relay[pl.ds(2 * i, 64, stride=BINS), :] = turned[:64]
        relay[pl.ds(2 * i + 1, 64, stride=BINS), :] = turned[64:]
        return 0

    lax.fori_loop(0, BINS // 2, turn_in, 0)

    for c in far:
        c.wait_recv()
    acc = chip_sum[...]
    for k in range(7):
        acc += z_in[k]
    total[...] = acc
    beside = [copy(total, total_l, 12, (right, me)), copy(total, total_r, 13, (left, me))]
    for c in beside:
        c.start()

    def to_operand(g, _):
        two = [relay[pl.ds(pl.multiple_of((2 * g + h) * BINS, 8), BINS), :] for h in range(2)]
        l_ref[g] = jnp.concatenate(two, axis=1).astype(BF16)
        return 0

    lax.fori_loop(0, GROUPS, to_operand, 0)
    for c in beside:
        c.wait_recv()

    half = iota((16, 128), 1) < OBS
    pl_, po, pr = total_l[...], total[...], total_r[...]
    first = jnp.where(half, pl_, lanes_roll(po, 64)), jnp.where(half, pr, 0.0)
    second = jnp.where(half, lanes_roll(pl_, 64), po), jnp.where(half, lanes_roll(pr, 64), 0.0)
    seen = jnp.concatenate([jnp.concatenate(first, axis=1), jnp.concatenate(second, axis=1)], axis=0)
    mean = jnp.sum(seen, axis=0, keepdims=True) * (1.0 / MEM)
    anomaly = (seen - mean) * metas[3:4]
    innovation = (metas[2:3] - mean) * metas[3:4]
    pulled = (anomaly * innovation)[:, :NEAR] * (1.0 / (MEM - 1))
    pull = folded(dot(stacked(pulled), taper_high)) + dot(pulled.astype(BF16), taper_low)
    pulls = stacked(pull)
    y_t = jnp.concatenate([anomaly] * 4, axis=0).T[:NEAR]
    y_t = jnp.concatenate([y_t, y_t], axis=1).astype(BF16)
    y = anomaly[:, :NEAR].astype(BF16)

    eye = (iota((MEM, PTS), 0) == iota((MEM, PTS), 1) % MEM).astype(F32)
    same = (iota((PTS, PTS), 0) // MEM == iota((PTS, PTS), 1) // MEM).astype(BF16)
    squares = []
    for g in range(OWN):
        matrix = eye + dot(y, w8[g] * y_t) * (1.0 / (MEM - 1))
        m_s[g] = matrix
        squares.append(jnp.sum(matrix * matrix, axis=0, keepdims=True))
        g_s[g] = folded(dot(pulls, expand[g]))
    norm = folded(dot(stacked(jnp.concatenate(squares, axis=0)), same))
    inv_scale = lax.rsqrt(norm)
    root_scale = jnp.sqrt(inv_scale)

    for it in range(NS_ITERS):
        for g in range(OWN):
            current = m_s[g] * inv_scale[g : g + 1] if it == 0 else m_s[g]
            step = 0.5 * (eye - current)
            operand = block_diagonal(step, same)
            if it == 0:
                moved = current + dot(current.astype(BF16), operand)
                z_s[g] = eye + step
            elif it == NS_ITERS - 1:
                inverse = z_s[g]
                z_s[g] = inverse + dot(inverse.astype(BF16), operand)
                continue
            else:
                inverse = z_s[g]
                both = dot(jnp.concatenate([current, inverse], axis=0).astype(BF16), operand)
                moved = current + both[:MEM]
                z_s[g] = inverse + both[MEM:]
            m_s[g] = moved + dot(moved.astype(BF16), operand)

    swaps = []
    for g in range(OWN):
        root = z_s[g] * root_scale[g : g + 1]
        half_step = jnp.sum(root * g_s[g], axis=0, keepdims=True)
        shift = folded(dot(stacked(root * half_step), same))
        mix = root + shift
        mix = mix + (1.0 - jnp.sum(mix, axis=0, keepdims=True)) * (1.0 / MEM)
        t_ref[core * OWN + g] = mix.astype(BF16)
        if g % 4 == 3:
            part = t_ref.at[pl.ds(core * OWN + g - 3, 4)]
            swap = copy(part, part, 14 + g // 4, (tile, mate))
            swap.start()
            swaps.append(swap)
    for c in swaps:
        c.wait()
    for c in halo + [pair] + far + beside:
        c.wait_send()


def combine_kernel(l_ref, t_ref, out_ref, relay):
    same = (iota((PTS, PTS), 0) // MEM == iota((PTS, PTS), 1) // MEM).astype(BF16)
    for g in range(GROUPS):
        mixed = dot(l_ref[g], block_diagonal(t_ref[g], same))
        for h in range(2):
            relay[(2 * g + h) * BINS : (2 * g + h + 1) * BINS, :] = mixed[:, 128 * h : 128 * h + 128]
    lane = iota((MEM, 128), 1)
    for i in range(BINS // 2):
        two = [relay[pl.ds(2 * i + k, 64, stride=BINS), :] for k in range(2)]
        turned = jnp.concatenate(two, axis=0).T
        q = [turned[MEM * k : MEM * (k + 1)] for k in range(4)]
        for h in range(2):
            a, b = q[2 * h], q[2 * h + 1]
            cut = slice(128 * h, 128 * h + 128)
            out_ref[2 * i, :, cut] = jnp.where(lane < 64, a, lanes_roll(b, 64)).astype(BF16)
            out_ref[2 * i + 1, :, cut] = jnp.where(lane < 64, lanes_roll(a, 64), b).astype(BF16)


def per_device(x, neighbors, obs_operator, obs_point, obs_type, obs_value, obs_var, obs_list, obs_count):
    theta = 2.0 * np.pi * (np.arange(BINS) % ND + 0.5) / ND
    cosine = jnp.asarray(np.broadcast_to(np.cos(theta)[:, None], (BINS, PTS)), F32)
    sine = jnp.asarray(np.broadcast_to(np.sin(theta)[:, None], (BINS, PTS)), F32)
    vmem = pl.BlockSpec(memory_space=pltpu.VMEM)
    tile_f32 = pltpu.VMEM((16, 128), F32)
    operand, transform = pl.pallas_call(
        exchange_kernel,
        out_shape=(
            jax.ShapeDtypeStruct((GROUPS, BINS, PTS), BF16),
            jax.ShapeDtypeStruct((GROUPS, MEM, PTS), BF16),
        ),
        in_specs=[vmem] * 11,
        out_specs=(vmem, vmem),
        scratch_shapes=[
            pltpu.VMEM((BINS, PTS), F32),
            pltpu.VMEM((BINS, PTS), F32),
            pltpu.VMEM((BINS, PTS), F32),
            pltpu.VMEM((SIX, MEM, 128), BF16),
            pltpu.VMEM((SIX, MEM, 128), BF16),
            pltpu.VMEM((SIX, MEM, 128), BF16),
            pltpu.VMEM((SIX, MEM, 128), BF16),
            pltpu.VMEM((8, 128), F32),
            pltpu.VMEM((8, 128), F32),
            pltpu.VMEM((8, 128), F32),
            pltpu.VMEM((BINS, MEM, PTS), BF16),
            tile_f32,
            tile_f32,
            tile_f32,
            pltpu.VMEM((7, 16, 128), F32),
            tile_f32,
            tile_f32,
            tile_f32,
            pltpu.VMEM((64 * BINS, 128), F32),
            pltpu.VMEM((OWN, NEAR, PTS), BF16),
            pltpu.VMEM((OWN, 128, PTS), BF16),
            pltpu.VMEM((OWN, MEM, PTS), F32),
            pltpu.VMEM((OWN, MEM, PTS), F32),
            pltpu.VMEM((OWN, MEM, PTS), F32),
            pltpu.SemaphoreType.DMA((18,)),
            pltpu.SemaphoreType.DMA((18,)),
        ],
        compiler_params=pltpu.CompilerParams(
            collective_id=0, has_side_effects=True, vmem_limit_bytes=40 << 20
        ),
        name="exchange",
    )(
        cosine, sine, x, neighbors, obs_operator, obs_point[None], obs_type[None], obs_value[None], obs_var[None],
        obs_list, obs_count[None],
    )
    return pl.pallas_call(
        combine_kernel,
        out_shape=jax.ShapeDtypeStruct((BINS, MEM, PTS), BF16),
        in_specs=[vmem, vmem],
        out_specs=vmem,
        scratch_shapes=[pltpu.VMEM((64 * BINS, 128), F32)],
        compiler_params=pltpu.CompilerParams(vmem_limit_bytes=40 << 20),
        name="combine",
    )(operand, transform)


def solution(mesh):
    placed = (
        P("bins", None, "space"),
        P(None, "space"),
        P(None, "bins"),
        P("space"),
        P("space"),
        P("space"),
        P("space"),
        P(None, "space"),
        P("space"),
    )
    return jax.shard_map(
        per_device, mesh=mesh, in_specs=placed, out_specs=P("bins", None, "space"), check_vma=False
    )
```

```python
import functools
import math

import jax
import jax.numpy as jnp
import numpy as np
from jax import lax
from jax.experimental import pallas as pl
from jax.experimental.pallas import tpu as pltpu
from jax.sharding import PartitionSpec as P

ND = 24
ROWS = 32
LOC_R = 6
NS_ITERS = 8
COURANT_MAX = 0.7
FREQ_RATIO = 1.1

BINS = 48
MEM = 32
PTS = 256
OBS = 64
NEAR = 3 * OBS
OWN = 16
GROUPS = 2 * OWN
TILES = 32
ZC = 8
SIX = 6
WEST = ((0, 0), (0, 3), (1, 0), (1, 3))
EAST = ((0, 1), (0, 2), (1, 1), (1, 2))

MESH = pl.DeviceIdType.MESH
F32 = jnp.float32
BF16 = jnp.bfloat16


def iota(shape, dim):
    return lax.broadcasted_iota(jnp.int32, shape, dim)


def dot(a, b):
    return jnp.dot(a, b, preferred_element_type=F32)


def split(a):
    high = a.astype(BF16)
    return high, (a - high.astype(F32)).astype(BF16)


def stacked(a):
    return jnp.concatenate(split(a), axis=0)


def folded(a):
    half = a.shape[0] // 2
    return a[:half] + a[half:]


def block_diagonal(rows, mask):
    return jnp.concatenate([rows.astype(BF16)] * 8, axis=0) * mask


def lanes_roll(a, by):
    return pltpu.roll(a, by % 128, 1)


def exchange_kernel(
    angle_in, x_in, nb_in, opw_in, opt_in, oty_in, oval_in, ovar_in, olist_in, ocnt_in,
    l_ref, t_ref,
    angle_ref, x_ref, nb_ref, opw_ref, opt_ref, oty_ref, oval_ref, ovar_ref, olist_ref, ocnt_ref,
    a1, a2, a3, send_w, send_e, recv_w, recv_e, meta, meta_l, meta_r, fore, sums, core_in, chip_sum, z_in,
    total, total_l, total_r, relay, w8, expand, m_s, z_s, g_s, lsem, ssem, rsem, ready,
):
    tile = lax.axis_index("space")
    me = lax.axis_index("bins")
    core = me % 2
    left, right = (tile + TILES - 1) % TILES, (tile + 1) % TILES
    mate = me + 1 - 2 * core

    def along(step):
        return (tile, (me + 2 * ZC + 2 * step) % (2 * ZC))

    barrier = pltpu.get_barrier_semaphore()
    partners = [(left, me), (right, me), along(1), along(-1), (tile, mate)]
    for who in partners:
        pl.semaphore_signal(barrier, inc=1, device_id=who, device_id_type=MESH)

    loads = [
        pltpu.make_async_copy(src, dst, lsem.at[n])
        for n, (src, dst) in enumerate(
            (
                (x_in, x_ref), (opt_in, opt_ref), (oval_in, oval_ref), (ovar_in, ovar_ref), (nb_in, nb_ref),
                (angle_in, angle_ref), (opw_in, opw_ref), (oty_in, oty_ref), (olist_in, olist_ref), (ocnt_in, ocnt_ref),
            )
        )
    ]
    for c in loads:
        c.start()

    def copy(src, dst, n, who):
        return pltpu.make_async_remote_copy(
            src_ref=src, dst_ref=dst, send_sem=ssem.at[n], recv_sem=rsem.at[n], device_id=who, device_id_type=MESH
        )

    lane = iota((MEM, 128), 1)
    block = lane // 32

    for c in loads[1:]:
        c.wait()
    zeros = jnp.zeros((1, OBS), F32)
    point = opt_ref[...]
    rows = [
        (point // ROWS).astype(F32), (point % ROWS).astype(F32), oval_ref[...], lax.rsqrt(ovar_ref[...]),
        zeros, zeros, zeros, zeros,
    ]
    packed = jnp.concatenate(rows, axis=0)
    meta[...] = jnp.concatenate([packed, jnp.zeros((8, OBS), F32)], axis=1)

    freq = (jnp.where(iota((BINS, PTS), 0) >= ND, 1, 0) + 2 * me).astype(F32)
    speed = COURANT_MAX * jnp.exp(-freq * math.log(FREQ_RATIO))
    open_side = (nb_ref[...] >= 0).astype(F32)
    cosine = jnp.concatenate([angle_ref[0]] * 2, axis=1)
    sine = jnp.concatenate([angle_ref[1]] * 2, axis=1)
    cx, cy = speed * jnp.abs(cosine), speed * jnp.abs(sine)
    a1[...] = 1.0 - cx - cy
    a2[...] = cx * jnp.where(cosine > 0, open_side[0:1], open_side[1:2])
    a3[...] = cy * jnp.where(sine > 0, open_side[2:3], open_side[3:4])

    here = (iota((PTS, OBS), 0) == point - tile * PTS).astype(BF16)
    kinds = (iota((16, OBS), 0) == oty_ref[...]).astype(F32)
    weights = lax.dot_general(
        opw_ref[...], kinds, (((0,), (0,)), ((), ())), precision=lax.Precision.HIGHEST, preferred_element_type=F32
    )

    def pack(j):
        for bins, buf, half, at in ((WEST, send_w, 1, 96), (EAST, send_e, 0, 0)):
            out = None
            for k, (f, q) in enumerate(bins):
                edge = x_ref[f * ND + q * SIX + j, :, 128 * half : 128 * half + 128].astype(F32)
                edge = lanes_roll(edge, 32 * k - at)
                out = edge if out is None else jnp.where(block == k, edge, out)
            buf[j] = out.astype(BF16)

    loads[0].wait()
    for j in range(SIX):
        pack(j)

    pl.semaphore_wait(barrier, len(partners))
    for step in (1, -1):
        pl.semaphore_signal(ready.at[0], inc=1, device_id=along(step), device_id_type=MESH)
    halo = [
        copy(send_w, recv_w, 0, (right, me)),
        copy(send_e, recv_e, 1, (left, me)),
        copy(meta, meta_l, 2, (right, me)),
        copy(meta, meta_r, 3, (left, me)),
    ]
    for c in halo:
        c.start()

    ids = jnp.where(iota((MEM, PTS), 0) < ocnt_ref[...], olist_ref[...] - (tile - 1) * OBS, -1)
    ids = jnp.where(olist_ref[...] >= 0, ids, -1)
    low, high = ids[:, :128], ids[:, 128:]
    low = jnp.where(core == 0, low, lanes_roll(low, -32))
    high = jnp.where(core == 0, high, lanes_roll(high, -32))
    ids = jnp.where(
        block == 0, low, jnp.where(block == 1, lanes_roll(low, -32), jnp.where(block == 2, lanes_roll(high, 64), lanes_roll(high, 32)))
    )
    number = iota((NEAR, 128), 0)
    used = jnp.zeros((NEAR, 128), F32)
    for slot in range(MEM):
        used = jnp.where(ids[slot : slot + 1] == number, 1.0, used)

    def upwind(j, f, q, inner):
        b = f * ND + q * SIX + j
        west = (f, q) in WEST
        mine = int(west == inner)
        halves = [x_ref[b, :, 128 * h : 128 * h + 128].astype(F32) for h in range(2)]
        here_x = halves[mine]
        if west:
            if inner:
                inflow = jnp.where(block == 0, lanes_roll(halves[0], 32), lanes_roll(halves[1], 32))
            else:
                edge = lanes_roll(recv_w[j].astype(F32), -32 * WEST.index((f, q)))
                inflow = jnp.where(block == 0, edge, lanes_roll(halves[0], 32))
        elif inner:
            inflow = jnp.where(block == 3, lanes_roll(halves[1], 96), lanes_roll(halves[0], 96))
        else:
            edge = lanes_roll(recv_e[j].astype(F32), 96 - 32 * EAST.index((f, q)))
            inflow = jnp.where(block == 3, edge, lanes_roll(halves[1], 96))
        beside_y = lanes_roll(here_x, 1 if q < 2 else 127)
        cut = slice(128 * mine, 128 * mine + 128)
        r1, r2, r3 = a1[b : b + 1, cut], a2[b : b + 1, cut], a3[b : b + 1, cut]
        fore[b, :, cut] = (here_x * r1 + inflow * r2 + beside_y * r3).astype(BF16)

    for j in range(SIX):
        for f in range(2):
            for q in range(4):
                upwind(j, f, q, True)

    pl.semaphore_wait(ready.at[0], 2)
    for step in (2, -2):
        pl.semaphore_signal(ready.at[1], inc=1, device_id=along(step), device_id_type=MESH)
    for c in halo:
        c.wait_recv()

    for j in range(SIX):
        for f in range(2):
            for q in range(4):
                upwind(j, f, q, False)

    predicted = jnp.zeros((MEM, OBS), F32)
    for part in range(4):
        at = dot(fore[12 * part : 12 * part + 12].reshape(12 * MEM, PTS), here)
        for i in range(12):
            b = 12 * part + i
            predicted += at[MEM * i : MEM * (i + 1)] * weights[b : b + 1]
    sums[...] = jnp.concatenate([predicted[:16], predicted[16:]], axis=1)
    pair = copy(sums, core_in, 4, (tile, mate))
    pair.start()

    metas = jnp.concatenate(
        [
            jnp.where(iota((8, 128), 1) < OBS, meta_l[...], lanes_roll(meta[...], 64)),
            jnp.where(iota((8, 128), 1) < OBS, meta_r[...], 0.0),
        ],
        axis=1,
    )
    places = jnp.concatenate([metas, jnp.zeros((120, PTS), F32)], axis=0).T
    own_lane = iota((NEAR, 128), 1)
    col = (tile * 8 + 2 * (own_lane // 32) + core).astype(F32)
    row = (own_lane % 32).astype(F32)
    distance = (places[:NEAR, 0:1] - col) ** 2 + (places[:NEAR, 1:2] - row) ** 2
    taper = (1.0 - distance / (2.0 * LOC_R * LOC_R)) ** 2 * used
    taper_high, taper_low = split(taper)

    big_lane = iota((128, PTS), 1)
    target = 32 * ((big_lane // 32) % 4) + big_lane // 128
    source = iota((128, PTS), 0)
    for g in range(OWN):
        spread = (source == target + 2 * g).astype(BF16)
        expand[g] = spread
        w8[g] = dot(taper_high, spread).astype(BF16)

    pair.wait_recv()
    pl.semaphore_wait(ready.at[1], 2)
    chip_sum[...] = sums[...] + core_in[...]
    far = [copy(chip_sum, z_in.at[k - 1], 4 + k, along(k)) for k in (4, 3, 5, 2, 6, 1, 7)]
    for c in far:
        c.start()

    def turn_in(i):
        f0, f1 = fore[2 * i].astype(F32), fore[2 * i + 1].astype(F32)
        parts = []
        for q in range(4):
            h = q // 2
            c0, c1 = f0[:, 128 * h : 128 * h + 128], f1[:, 128 * h : 128 * h + 128]
            if q % 2 == 0:
                parts.append(jnp.where(lane < 64, c0, lanes_roll(c1, 64)))
            else:
                parts.append(jnp.where(lane < 64, lanes_roll(c0, 64), c1))
        turned = jnp.concatenate(parts, axis=0).T
        relay[pl.ds(2 * i, 64, stride=BINS), :] = turned[:64]
        relay[pl.ds(2 * i + 1, 64, stride=BINS), :] = turned[64:]

    for i in range(BINS // 2):
        turn_in(i)

    for g in range(GROUPS):
        two = [relay[(2 * g + h) * BINS : (2 * g + h + 1) * BINS, :] for h in range(2)]
        l_ref[g] = jnp.concatenate(two, axis=1).astype(BF16)

    for c in far:
        c.wait_recv()
    acc = chip_sum[...]
    for k in range(7):
        acc += z_in[k]
    total[...] = acc
    beside = [copy(total, total_l, 12, (right, me)), copy(total, total_r, 13, (left, me))]
    for c in beside:
        c.start()

    for c in beside:
        c.wait_recv()

    half = iota((16, 128), 1) < OBS
    pl_, po, pr = total_l[...], total[...], total_r[...]
    first = jnp.where(half, pl_, lanes_roll(po, 64)), jnp.where(half, pr, 0.0)
    second = jnp.where(half, lanes_roll(pl_, 64), po), jnp.where(half, lanes_roll(pr, 64), 0.0)
    seen = jnp.concatenate([jnp.concatenate(first, axis=1), jnp.concatenate(second, axis=1)], axis=0)
    mean = jnp.sum(seen, axis=0, keepdims=True) * (1.0 / MEM)
    anomaly = (seen - mean) * metas[3:4]
    innovation = (metas[2:3] - mean) * metas[3:4]
    pulled = (anomaly * innovation)[:, :NEAR] * (1.0 / (MEM - 1))
    pull = folded(dot(stacked(pulled), taper_high)) + dot(pulled.astype(BF16), taper_low)
    pulls = stacked(pull)
    y_t = jnp.concatenate([anomaly] * 4, axis=0).T[:NEAR]
    y_t = jnp.concatenate([y_t, y_t], axis=1).astype(BF16)
    y = anomaly[:, :NEAR].astype(BF16)

    eye = (iota((MEM, PTS), 0) == iota((MEM, PTS), 1) % MEM).astype(F32)
    same = (iota((PTS, PTS), 0) // MEM == iota((PTS, PTS), 1) // MEM).astype(BF16)
    squares = []
    for g in range(OWN):
        matrix = eye + dot(y, w8[g] * y_t) * (1.0 / (MEM - 1))
        m_s[g] = matrix
        squares.append(jnp.sum(matrix * matrix, axis=0, keepdims=True))
        g_s[g] = folded(dot(pulls, expand[g]))
    norm = folded(dot(stacked(jnp.concatenate(squares, axis=0)), same))
    inv_scale = lax.rsqrt(norm)
    root_scale = jnp.sqrt(inv_scale)

    for it in range(NS_ITERS):
        for g in range(OWN):
            current = m_s[g] * inv_scale[g : g + 1] if it == 0 else m_s[g]
            step = 0.5 * (eye - current)
            operand = block_diagonal(step, same)
            if it == 0:
                moved = current + dot(current.astype(BF16), operand)
                z_s[g] = eye + step
            elif it == NS_ITERS - 1:
                inverse = z_s[g]
                z_s[g] = inverse + dot(inverse.astype(BF16), operand)
                continue
            else:
                inverse = z_s[g]
                both = dot(jnp.concatenate([current, inverse], axis=0).astype(BF16), operand)
                moved = current + both[:MEM]
                z_s[g] = inverse + both[MEM:]
            m_s[g] = moved + dot(moved.astype(BF16), operand)

    swaps = []
    for g in range(OWN):
        root = z_s[g] * root_scale[g : g + 1]
        half_step = jnp.sum(root * g_s[g], axis=0, keepdims=True)
        shift = folded(dot(stacked(root * half_step), same))
        mix = root + shift
        mix = mix + (1.0 - jnp.sum(mix, axis=0, keepdims=True)) * (1.0 / MEM)
        t_ref[core * OWN + g] = mix.astype(BF16)
        if g % 4 == 3:
            part = t_ref.at[pl.ds(core * OWN + g - 3, 4)]
            swap = copy(part, part, 14 + g // 4, (tile, mate))
            swap.start()
            swaps.append(swap)
    for c in swaps:
        c.wait()
    for c in halo + [pair] + far + beside:
        c.wait_send()


def combine_kernel(l_ref, t_ref, out_ref, relay):
    same = (iota((PTS, PTS), 0) // MEM == iota((PTS, PTS), 1) // MEM).astype(BF16)
    for g in range(GROUPS):
        mixed = dot(l_ref[g], block_diagonal(t_ref[g], same))
        for h in range(2):
            relay[(2 * g + h) * BINS : (2 * g + h + 1) * BINS, :] = mixed[:, 128 * h : 128 * h + 128]
    lane = iota((MEM, 128), 1)
    for i in range(BINS // 2):
        two = [relay[pl.ds(2 * i + k, 64, stride=BINS), :] for k in range(2)]
        turned = jnp.concatenate(two, axis=0).T
        q = [turned[MEM * k : MEM * (k + 1)] for k in range(4)]
        for h in range(2):
            a, b = q[2 * h], q[2 * h + 1]
            cut = slice(128 * h, 128 * h + 128)
            out_ref[2 * i, :, cut] = jnp.where(lane < 64, a, lanes_roll(b, 64)).astype(BF16)
            out_ref[2 * i + 1, :, cut] = jnp.where(lane < 64, lanes_roll(a, 64), b).astype(BF16)


def per_device(x, neighbors, obs_operator, obs_point, obs_type, obs_value, obs_var, obs_list, obs_count):
    theta = 2.0 * np.pi * (np.arange(BINS) % ND + 0.5) / ND
    angles = np.stack([np.cos(theta), np.sin(theta)])[:, :, None]
    angles = jnp.asarray(np.broadcast_to(angles, (2, BINS, 128)), F32)
    vmem = pl.BlockSpec(memory_space=pltpu.VMEM)
    tile_f32 = pltpu.VMEM((16, 128), F32)
    operands = (
        angles, x, neighbors, obs_operator, obs_point[None], obs_type[None], obs_value[None], obs_var[None],
        obs_list, obs_count[None],
    )
    operands = [pltpu.with_memory_space_constraint(a, pltpu.HBM) for a in operands]
    operand, transform = pl.pallas_call(
        exchange_kernel,
        out_shape=(
            jax.ShapeDtypeStruct((GROUPS, BINS, PTS), BF16),
            jax.ShapeDtypeStruct((GROUPS, MEM, PTS), BF16),
        ),
        in_specs=[pl.BlockSpec(memory_space=pltpu.HBM)] * 10,
        out_specs=(vmem, vmem),
        scratch_shapes=[
            pltpu.VMEM((2, BINS, 128), F32),
            pltpu.VMEM((BINS, MEM, PTS), BF16),
            pltpu.VMEM((4, PTS), jnp.int32),
            pltpu.VMEM((16, BINS), F32),
            pltpu.VMEM((1, OBS), jnp.int32),
            pltpu.VMEM((1, OBS), jnp.int32),
            pltpu.VMEM((1, OBS), F32),
            pltpu.VMEM((1, OBS), F32),
            pltpu.VMEM((MEM, PTS), jnp.int32),
            pltpu.VMEM((1, PTS), jnp.int32),
            pltpu.VMEM((BINS, PTS), F32),
            pltpu.VMEM((BINS, PTS), F32),
            pltpu.VMEM((BINS, PTS), F32),
            pltpu.VMEM((SIX, MEM, 128), BF16),
            pltpu.VMEM((SIX, MEM, 128), BF16),
            pltpu.VMEM((SIX, MEM, 128), BF16),
            pltpu.VMEM((SIX, MEM, 128), BF16),
            pltpu.VMEM((8, 128), F32),
            pltpu.VMEM((8, 128), F32),
            pltpu.VMEM((8, 128), F32),
            pltpu.VMEM((BINS, MEM, PTS), BF16),
            tile_f32,
            tile_f32,
            tile_f32,
            pltpu.VMEM((7, 16, 128), F32),
            tile_f32,
            tile_f32,
            tile_f32,
            pltpu.VMEM((64 * BINS, 128), F32),
            pltpu.VMEM((OWN, NEAR, PTS), BF16),
            pltpu.VMEM((OWN, 128, PTS), BF16),
            pltpu.VMEM((OWN, MEM, PTS), F32),
            pltpu.VMEM((OWN, MEM, PTS), F32),
            pltpu.VMEM((OWN, MEM, PTS), F32),
            pltpu.SemaphoreType.DMA((10,)),
            pltpu.SemaphoreType.DMA((18,)),
            pltpu.SemaphoreType.DMA((18,)),
            pltpu.SemaphoreType.REGULAR((2,)),
        ],
        compiler_params=pltpu.CompilerParams(
            collective_id=0, has_side_effects=True, vmem_limit_bytes=40 << 20
        ),
        name="exchange",
    )(*operands)
    return pl.pallas_call(
        combine_kernel,
        out_shape=jax.ShapeDtypeStruct((BINS, MEM, PTS), BF16),
        in_specs=[vmem, vmem],
        out_specs=vmem,
        scratch_shapes=[pltpu.VMEM((64 * BINS, 128), F32)],
        compiler_params=pltpu.CompilerParams(vmem_limit_bytes=40 << 20),
        name="combine",
    )(operand, transform)


def solution(mesh):
    placed = (
        P("bins", None, "space"),
        P(None, "space"),
        P(None, "bins"),
        P("space"),
        P("space"),
        P("space"),
        P("space"),
        P(None, "space"),
        P("space"),
    )
    return jax.shard_map(
        per_device, mesh=mesh, in_specs=placed, out_specs=P("bins", None, "space"), check_vma=False
    )
```

```python
import functools
import math

import jax
import jax.numpy as jnp
import numpy as np
from jax import lax
from jax.experimental import pallas as pl
from jax.experimental.pallas import tpu as pltpu
from jax.sharding import PartitionSpec as P

ND = 24
ROWS = 32
LOC_R = 6
NS_ITERS = 8
COURANT_MAX = 0.7
FREQ_RATIO = 1.1

BINS = 48
MEM = 32
PTS = 256
OBS = 64
NEAR = 3 * OBS
OWN = 16
GROUPS = 2 * OWN
TILES = 32
ZC = 8
SIX = 6
WEST = ((0, 0), (0, 3), (1, 0), (1, 3))
EAST = ((0, 1), (0, 2), (1, 1), (1, 2))

MESH = pl.DeviceIdType.MESH
F32 = jnp.float32
BF16 = jnp.bfloat16


def iota(shape, dim):
    return lax.broadcasted_iota(jnp.int32, shape, dim)


def dot(a, b):
    return jnp.dot(a, b, preferred_element_type=F32)


def split(a):
    high = a.astype(BF16)
    return high, (a - high.astype(F32)).astype(BF16)


def stacked(a):
    return jnp.concatenate(split(a), axis=0)


def folded(a):
    half = a.shape[0] // 2
    return a[:half] + a[half:]


def block_diagonal(rows, mask):
    return jnp.concatenate([rows.astype(BF16)] * (mask.shape[0] // MEM), axis=0) * mask


def lanes_roll(a, by):
    return pltpu.roll(a, by % 128, 1)


def exchange_kernel(
    angle_in, x_in, nb_in, opw_in, opt_in, oty_in, oval_in, ovar_in, olist_in, ocnt_in,
    mixed_ref,
    angle_ref, x_ref, nb_ref, opw_ref, opt_ref, oty_ref, oval_ref, ovar_ref, olist_ref, ocnt_ref,
    a1, a2, a3, send_w, send_e, recv_w, recv_e, edge_w, edge_e, meta, meta_l, meta_r, fore, sums, z_in, total, total_m,
    total_l, total_r, relay, operand, w8, expand, m_s, z_s, g_s, t_own, t_in, lsem, ssem, rsem, ready,
):
    tile = lax.axis_index("space")
    me = lax.axis_index("bins")
    core = me % 2
    left, right = (tile + TILES - 1) % TILES, (tile + 1) % TILES
    mate = me + 1 - 2 * core

    def along(step):
        return (tile, (me + 2 * ZC + 2 * step) % (2 * ZC))

    barrier = pltpu.get_barrier_semaphore()
    partners = [(left, me), (right, me), (left, mate), (right, mate), (tile, mate), along(1), along(-1)]
    for who in partners:
        pl.semaphore_signal(barrier, inc=1, device_id=who, device_id_type=MESH)

    loads = [
        pltpu.make_async_copy(src, dst, lsem.at[n])
        for n, (src, dst) in enumerate(
            (
                (x_in, x_ref), (opt_in, opt_ref), (oval_in, oval_ref), (ovar_in, ovar_ref), (nb_in, nb_ref),
                (angle_in, angle_ref), (opw_in, opw_ref), (oty_in, oty_ref), (olist_in, olist_ref), (ocnt_in, ocnt_ref),
            )
        )
    ]
    for c in loads:
        c.start()

    def copy(src, dst, n, who):
        return pltpu.make_async_remote_copy(
            src_ref=src, dst_ref=dst, send_sem=ssem.at[n], recv_sem=rsem.at[n], device_id=who, device_id_type=MESH
        )

    lane = iota((MEM, 128), 1)
    block = lane // 32

    for c in loads[1:]:
        c.wait()
    zeros = jnp.zeros((1, OBS), F32)
    point = opt_ref[...]
    rows = [
        (point // ROWS).astype(F32), (point % ROWS).astype(F32), oval_ref[...], lax.rsqrt(ovar_ref[...]),
        zeros, zeros, zeros, zeros,
    ]
    packed = jnp.concatenate(rows, axis=0)
    meta[...] = jnp.concatenate([packed, jnp.zeros((8, OBS), F32)], axis=1)

    freq = (jnp.where(iota((BINS, PTS), 0) >= ND, 1, 0) + 2 * me).astype(F32)
    speed = COURANT_MAX * jnp.exp(-freq * math.log(FREQ_RATIO))
    open_side = (nb_ref[...] >= 0).astype(F32)
    cosine = jnp.concatenate([angle_ref[0]] * 2, axis=1)
    sine = jnp.concatenate([angle_ref[1]] * 2, axis=1)
    cx, cy = speed * jnp.abs(cosine), speed * jnp.abs(sine)
    a1[...] = 1.0 - cx - cy
    a2[...] = cx * jnp.where(cosine > 0, open_side[0:1], open_side[1:2])
    a3[...] = cy * jnp.where(sine > 0, open_side[2:3], open_side[3:4])

    here = (iota((PTS, OBS), 0) == point - tile * PTS).astype(BF16)
    kinds = (iota((16, OBS), 0) == oty_ref[...]).astype(F32)
    weights = lax.dot_general(
        opw_ref[...], kinds, (((0,), (0,)), ((), ())), precision=lax.Precision.HIGHEST, preferred_element_type=F32
    )

    at_obs = dot(jnp.concatenate([open_side, jnp.zeros((4, PTS), F32)], axis=0).astype(BF16), here)
    obs_col, obs_row = point // ROWS - tile * (PTS // ROWS), point % ROWS
    first_col = jnp.where(obs_col == 0, at_obs[0:1], 0.0)
    last_col = jnp.where(obs_col == PTS // ROWS - 1, at_obs[1:2], 0.0)
    in_row = (iota((ROWS, OBS), 0) == obs_row).astype(F32)
    carried = weights * cx[:, :OBS]
    for j in range(SIX):
        for bins, buf, on in ((WEST, edge_w, first_col), (EAST, edge_e, last_col)):
            rows4 = [in_row * (carried[f * ND + q * SIX + j : f * ND + q * SIX + j + 1] * on) for f, q in bins]
            buf[j] = jnp.concatenate(rows4, axis=0).astype(BF16)

    def pack(j):
        for bins, buf, half, at in ((WEST, send_w, 1, 96), (EAST, send_e, 0, 0)):
            out = None
            for k, (f, q) in enumerate(bins):
                edge = x_ref[f * ND + q * SIX + j, :, 128 * half : 128 * half + 128].astype(F32)
                edge = lanes_roll(edge, 32 * k - at)
                out = edge if out is None else jnp.where(block == k, edge, out)
            buf[j] = out.astype(BF16)

    loads[0].wait()
    for j in range(SIX):
        pack(j)

    pl.semaphore_wait(barrier, len(partners))
    for step in (1, -1):
        pl.semaphore_signal(ready.at[0], inc=1, device_id=along(step), device_id_type=MESH)
    halo = [
        copy(send_w, recv_w, 0, (right, me)),
        copy(send_e, recv_e, 1, (left, me)),
        copy(meta, meta_l, 2, (right, me)),
        copy(meta, meta_r, 3, (left, me)),
    ]
    for c in halo:
        c.start()

    def upwind(j, f, q, part):
        b = f * ND + q * SIX + j
        west = (f, q) in WEST
        mine = int(west == (part == 0))
        halves = [x_ref[b, :, 128 * h : 128 * h + 128].astype(F32) for h in range(2)]
        here_x = halves[mine]
        if part == 2:
            spot = (WEST if west else EAST).index((f, q))
            edge = (recv_w if west else recv_e)[j].astype(F32)
            edge = lanes_roll(edge, (0 if west else 96) - 32 * spot)
        else:
            edge = jnp.zeros((MEM, 128), F32)
        if west:
            other = lanes_roll(halves[0], 32) if part == 0 else edge
            inflow = jnp.where(block == 0, other, lanes_roll(here_x, 32))
        else:
            other = lanes_roll(halves[1], 96) if part == 0 else edge
            inflow = jnp.where(block == 3, other, lanes_roll(here_x, 96))
        beside_y = lanes_roll(here_x, 1 if q < 2 else 127)
        cut = slice(128 * mine, 128 * mine + 128)
        r1, r2, r3 = a1[b : b + 1, cut], a2[b : b + 1, cut], a3[b : b + 1, cut]
        fore[b, :, cut] = (here_x * r1 + inflow * r2 + beside_y * r3).astype(BF16)

    def upwind_all(*parts):
        for j in range(SIX):
            for f in range(2):
                for q in range(4):
                    for part in parts:
                        upwind(j, f, q, part)

    upwind_all(0, 1)

    predicted = jnp.zeros((MEM, OBS), F32)
    for part in range(4):
        at = dot(fore[12 * part : 12 * part + 12].reshape(12 * MEM, PTS), here)
        for i in range(12):
            b = 12 * part + i
            predicted += at[MEM * i : MEM * (i + 1)] * weights[b : b + 1]

    pl.semaphore_wait(ready.at[0], 2)
    for step in (2, -2):
        pl.semaphore_signal(ready.at[1], inc=1, device_id=along(step), device_id_type=MESH)

    ids = jnp.where(iota((MEM, PTS), 0) < ocnt_ref[...], olist_ref[...] - (tile - 1) * OBS, -1)
    ids = jnp.where(olist_ref[...] >= 0, ids, -1)
    low, high = ids[:, :128], ids[:, 128:]
    low = jnp.where(core == 0, low, lanes_roll(low, -32))
    high = jnp.where(core == 0, high, lanes_roll(high, -32))
    ids = jnp.where(
        block == 0, low, jnp.where(block == 1, lanes_roll(low, -32), jnp.where(block == 2, lanes_roll(high, 64), lanes_roll(high, 32)))
    )
    number = iota((NEAR, 128), 0)
    used = jnp.zeros((NEAR, 128), F32)
    for slot in range(MEM):
        used = jnp.where(ids[slot : slot + 1] == number, 1.0, used)

    halo[0].wait_recv()
    halo[1].wait_recv()
    for j in range(SIX):
        predicted += dot(recv_w[j], edge_w[j]) + dot(recv_e[j], edge_e[j])
    sums[...] = jnp.concatenate([predicted[:16], predicted[16:]], axis=1)
    pl.semaphore_wait(ready.at[1], 2)
    far = [copy(sums, z_in.at[k - 1], 4 + k, along(k)) for k in (1, 7, 2, 6, 3, 5, 4)]
    for c in far:
        c.start()
    halo[2].wait_recv()
    halo[3].wait_recv()

    metas = jnp.concatenate(
        [
            jnp.where(iota((8, 128), 1) < OBS, meta_l[...], lanes_roll(meta[...], 64)),
            jnp.where(iota((8, 128), 1) < OBS, meta_r[...], 0.0),
        ],
        axis=1,
    )
    places = jnp.concatenate([metas, jnp.zeros((120, PTS), F32)], axis=0).T
    own_lane = iota((NEAR, 128), 1)
    col = (tile * 8 + 2 * (own_lane // 32) + core).astype(F32)
    row = (own_lane % 32).astype(F32)
    distance = (places[:NEAR, 0:1] - col) ** 2 + (places[:NEAR, 1:2] - row) ** 2
    taper = (1.0 - distance / (2.0 * LOC_R * LOC_R)) ** 2 * used
    taper_high, taper_low = split(taper)

    big_lane = iota((128, PTS), 1)
    target = 32 * ((big_lane // 32) % 4) + big_lane // 128
    source = iota((128, PTS), 0)
    for g in range(OWN):
        spread = (source == target + 2 * g).astype(BF16)
        expand[g] = spread
        w8[g] = dot(taper_high, spread).astype(BF16)

    upwind_all(2)

    def turn_in(i):
        f0, f1 = fore[2 * i].astype(F32), fore[2 * i + 1].astype(F32)
        parts = []
        for q in range(4):
            h = q // 2
            c0, c1 = f0[:, 128 * h : 128 * h + 128], f1[:, 128 * h : 128 * h + 128]
            if q % 2 == 0:
                parts.append(jnp.where(lane < 64, c0, lanes_roll(c1, 64)))
            else:
                parts.append(jnp.where(lane < 64, lanes_roll(c0, 64), c1))
        turned = jnp.concatenate(parts, axis=0).T
        relay[pl.ds(2 * i, 64, stride=BINS), :] = turned[:64]
        relay[pl.ds(2 * i + 1, 64, stride=BINS), :] = turned[64:]

    for i in range(BINS // 2):
        turn_in(i)

    for t in range(2 * GROUPS):
        operand[t] = relay[t * BINS : (t + 1) * BINS, :].astype(BF16)

    for c in far:
        c.wait_recv()
    acc = sums[...]
    for k in range(7):
        acc += z_in[k]
    total[...] = acc
    beside = [
        copy(total, total_l.at[0], 12, (right, me)),
        copy(total, total_r.at[0], 13, (left, me)),
        copy(total, total_l.at[1], 14, (right, mate)),
        copy(total, total_r.at[1], 15, (left, mate)),
        copy(total, total_m, 16, (tile, mate)),
    ]
    for c in beside:
        c.start()
    for c in beside:
        c.wait_recv()

    half = iota((16, 128), 1) < OBS
    pl_, po, pr = total_l[0] + total_l[1], total[...] + total_m[...], total_r[0] + total_r[1]
    first = jnp.where(half, pl_, lanes_roll(po, 64)), jnp.where(half, pr, 0.0)
    second = jnp.where(half, lanes_roll(pl_, 64), po), jnp.where(half, lanes_roll(pr, 64), 0.0)
    seen = jnp.concatenate([jnp.concatenate(first, axis=1), jnp.concatenate(second, axis=1)], axis=0)
    mean = jnp.sum(seen, axis=0, keepdims=True) * (1.0 / MEM)
    anomaly = (seen - mean) * metas[3:4]
    innovation = (metas[2:3] - mean) * metas[3:4]
    pulled = (anomaly * innovation)[:, :NEAR] * (1.0 / (MEM - 1))
    pull = folded(dot(stacked(pulled), taper_high)) + dot(pulled.astype(BF16), taper_low)
    pulls = stacked(pull)
    y_t = jnp.concatenate([anomaly] * 4, axis=0).T[:NEAR]
    y_t = jnp.concatenate([y_t, y_t], axis=1).astype(BF16)
    y = anomaly[:, :NEAR].astype(BF16)

    eye = (iota((MEM, PTS), 0) == iota((MEM, PTS), 1) % MEM).astype(F32)
    same = (iota((PTS, PTS), 0) // MEM == iota((PTS, PTS), 1) // MEM).astype(BF16)
    squares = []
    for g in range(OWN):
        matrix = eye + dot(y, w8[g] * y_t) * (1.0 / (MEM - 1))
        m_s[g] = matrix
        squares.append(jnp.sum(matrix * matrix, axis=0, keepdims=True))
        g_s[g] = folded(dot(pulls, expand[g]))
    norm = folded(dot(stacked(jnp.concatenate(squares, axis=0)), same))
    inv_scale = lax.rsqrt(norm)
    root_scale = jnp.sqrt(inv_scale)

    same_half = same[:128, :128]
    for it in range(NS_ITERS):
        for g in range(OWN):
            for h in range(2):
                cut = slice(128 * h, 128 * h + 128)
                current = m_s[g, :, cut]
                if it == 0:
                    current = current * inv_scale[g : g + 1, cut]
                step = 0.5 * (eye[:, cut] - current)
                weight = block_diagonal(step, same_half)
                if it == 0:
                    moved = current + dot(current.astype(BF16), weight)
                    z_s[g, :, cut] = eye[:, cut] + step
                elif it == NS_ITERS - 1:
                    inverse = z_s[g, :, cut]
                    z_s[g, :, cut] = inverse + dot(inverse.astype(BF16), weight)
                    continue
                else:
                    inverse = z_s[g, :, cut]
                    both = dot(jnp.concatenate([current, inverse], axis=0).astype(BF16), weight)
                    moved = current + both[:MEM]
                    z_s[g, :, cut] = inverse + both[MEM:]
                m_s[g, :, cut] = moved + dot(moved.astype(BF16), weight)

    swaps = []
    for g in range(OWN):
        root = z_s[g] * root_scale[g : g + 1]
        half_step = jnp.sum(root * g_s[g], axis=0, keepdims=True)
        shift = folded(dot(stacked(root * half_step), same))
        mix = root + shift
        mix = mix + (1.0 - jnp.sum(mix, axis=0, keepdims=True)) * (1.0 / MEM)
        t_own[g] = mix.astype(BF16)
        if g % 4 == 3:
            part = pl.ds(g - 3, 4)
            swap = copy(t_own.at[part], t_in.at[part], 17 + g // 4, (tile, mate))
            swap.start()
            swaps.append(swap)

    def apply(owner, g, transform):
        for h in range(2):
            t = 2 * OWN * owner + 2 * g + h
            weight = block_diagonal(transform[g, :, 128 * h : 128 * h + 128], same_half)
            mixed_ref[pl.ds(pl.multiple_of(t * BINS, 8), BINS), :] = dot(operand[t], weight)

    for g in range(OWN):
        apply(core, g, t_own)
    for n, c in enumerate(swaps):
        c.wait_recv()
        for g in range(4 * n, 4 * n + 4):
            apply(1 - core, g, t_in)
    for c in halo + far + beside + swaps:
        c.wait_send()


def place_kernel(mixed_ref, out_hbm, out_ref, sem):
    lane = iota((MEM, 128), 1)
    copies = []
    for i in range(BINS // 2):
        two = [mixed_ref[pl.ds(2 * i + k, 64, stride=BINS), :] for k in range(2)]
        turned = jnp.concatenate(two, axis=0).T
        q = [turned[MEM * k : MEM * (k + 1)] for k in range(4)]
        for h in range(2):
            a, b = q[2 * h], q[2 * h + 1]
            cut = slice(128 * h, 128 * h + 128)
            out_ref[2 * i, :, cut] = jnp.where(lane < 64, a, lanes_roll(b, 64)).astype(BF16)
            out_ref[2 * i + 1, :, cut] = jnp.where(lane < 64, lanes_roll(a, 64), b).astype(BF16)
        if i % 4 == 3:
            part = pl.ds(2 * i - 6, 8)
            c = pltpu.make_async_copy(out_ref.at[part], out_hbm.at[part], sem.at[i // 4])
            c.start()
            copies.append(c)
    for c in copies:
        c.wait()


def per_device(x, neighbors, obs_operator, obs_point, obs_type, obs_value, obs_var, obs_list, obs_count):
    theta = 2.0 * np.pi * (np.arange(BINS) % ND + 0.5) / ND
    angles = np.stack([np.cos(theta), np.sin(theta)])[:, :, None]
    angles = jnp.asarray(np.broadcast_to(angles, (2, BINS, 128)), F32)
    vmem = pl.BlockSpec(memory_space=pltpu.VMEM)
    tile_f32 = pltpu.VMEM((16, 128), F32)
    operands = (
        angles, x, neighbors, obs_operator, obs_point[None], obs_type[None], obs_value[None], obs_var[None],
        obs_list, obs_count[None],
    )
    operands = [pltpu.with_memory_space_constraint(a, pltpu.HBM) for a in operands]
    mixed = pl.pallas_call(
        exchange_kernel,
        out_shape=jax.ShapeDtypeStruct((2 * GROUPS * BINS, 128), F32),
        in_specs=[pl.BlockSpec(memory_space=pltpu.HBM)] * 10,
        out_specs=vmem,
        scratch_shapes=[
            pltpu.VMEM((2, BINS, 128), F32),
            pltpu.VMEM((BINS, MEM, PTS), BF16),
            pltpu.VMEM((4, PTS), jnp.int32),
            pltpu.VMEM((16, BINS), F32),
            pltpu.VMEM((1, OBS), jnp.int32),
            pltpu.VMEM((1, OBS), jnp.int32),
            pltpu.VMEM((1, OBS), F32),
            pltpu.VMEM((1, OBS), F32),
            pltpu.VMEM((MEM, PTS), jnp.int32),
            pltpu.VMEM((1, PTS), jnp.int32),
            pltpu.VMEM((BINS, PTS), F32),
            pltpu.VMEM((BINS, PTS), F32),
            pltpu.VMEM((BINS, PTS), F32),
            pltpu.VMEM((SIX, MEM, 128), BF16),
            pltpu.VMEM((SIX, MEM, 128), BF16),
            pltpu.VMEM((SIX, MEM, 128), BF16),
            pltpu.VMEM((SIX, MEM, 128), BF16),
            pltpu.VMEM((SIX, 128, OBS), BF16),
            pltpu.VMEM((SIX, 128, OBS), BF16),
            pltpu.VMEM((8, 128), F32),
            pltpu.VMEM((8, 128), F32),
            pltpu.VMEM((8, 128), F32),
            pltpu.VMEM((BINS, MEM, PTS), BF16),
            tile_f32,
            pltpu.VMEM((7, 16, 128), F32),
            tile_f32,
            tile_f32,
            pltpu.VMEM((2, 16, 128), F32),
            pltpu.VMEM((2, 16, 128), F32),
            pltpu.VMEM((64 * BINS, 128), F32),
            pltpu.VMEM((2 * GROUPS, BINS, 128), BF16),
            pltpu.VMEM((OWN, NEAR, PTS), BF16),
            pltpu.VMEM((OWN, 128, PTS), BF16),
            pltpu.VMEM((OWN, MEM, PTS), F32),
            pltpu.VMEM((OWN, MEM, PTS), F32),
            pltpu.VMEM((OWN, MEM, PTS), F32),
            pltpu.VMEM((OWN, MEM, PTS), BF16),
            pltpu.VMEM((OWN, MEM, PTS), BF16),
            pltpu.SemaphoreType.DMA((10,)),
            pltpu.SemaphoreType.DMA((21,)),
            pltpu.SemaphoreType.DMA((21,)),
            pltpu.SemaphoreType.REGULAR((2,)),
        ],
        compiler_params=pltpu.CompilerParams(
            collective_id=0, has_side_effects=True, vmem_limit_bytes=40 << 20
        ),
        name="exchange",
    )(*operands)
    return pl.pallas_call(
        place_kernel,
        out_shape=jax.ShapeDtypeStruct((BINS, MEM, PTS), BF16),
        in_specs=[vmem],
        out_specs=pl.BlockSpec(memory_space=pl.ANY),
        scratch_shapes=[pltpu.VMEM((BINS, MEM, PTS), BF16), pltpu.SemaphoreType.DMA((SIX,))],
        compiler_params=pltpu.CompilerParams(vmem_limit_bytes=40 << 20),
        name="place",
    )(mixed)


def solution(mesh):
    placed = (
        P("bins", None, "space"),
        P(None, "space"),
        P(None, "bins"),
        P("space"),
        P("space"),
        P("space"),
        P("space"),
        P(None, "space"),
        P("space"),
    )
    return jax.shard_map(
        per_device, mesh=mesh, in_specs=placed, out_specs=P("bins", None, "space"), check_vma=False
    )
```

```python
import functools
import math

import jax
import jax.numpy as jnp
import numpy as np
from jax import lax
from jax.experimental import pallas as pl
from jax.experimental.pallas import tpu as pltpu
from jax.sharding import PartitionSpec as P

ND = 24
ROWS = 32
LOC_R = 6
NS_ITERS = 8
COURANT_MAX = 0.7
FREQ_RATIO = 1.1

BINS = 48
MEM = 32
PTS = 256
OBS = 64
NEAR = 3 * OBS
OWN = 16
GROUPS = 2 * OWN
TILES = 32
ZC = 8
BATCHES = (range(8), range(8, 16))
SENT = (0, 8, 12, 16)
SIX = 6
WEST = ((0, 0), (0, 3), (1, 0), (1, 3))
EAST = ((0, 1), (0, 2), (1, 1), (1, 2))

MESH = pl.DeviceIdType.MESH
F32 = jnp.float32
BF16 = jnp.bfloat16


def iota(shape, dim):
    return lax.broadcasted_iota(jnp.int32, shape, dim)


def dot(a, b):
    return jnp.dot(a, b, preferred_element_type=F32)


def split(a):
    high = a.astype(BF16)
    return high, (a - high.astype(F32)).astype(BF16)


def stacked(a):
    return jnp.concatenate(split(a), axis=0)


def folded(a):
    half = a.shape[0] // 2
    return a[:half] + a[half:]


def block_diagonal(rows, mask):
    return jnp.concatenate([rows.astype(BF16)] * (mask.shape[0] // MEM), axis=0) * mask


def lanes_roll(a, by):
    return pltpu.roll(a, by % 128, 1)


def exchange_kernel(
    angle_in, x_in, nb_in, opw_in, opt_in, oty_in, oval_in, ovar_in, olist_in, ocnt_in,
    mixed_ref,
    angle_ref, x_ref, nb_ref, opw_ref, opt_ref, oty_ref, oval_ref, ovar_ref, olist_ref, ocnt_ref,
    a1, a2, a3, send_w, send_e, recv_w, recv_e, edge_w, edge_e, meta, meta_l, meta_r, fore, sums, z_in, total, total_m,
    total_l, total_r, relay, operand, w8, expand, m_s, z_s, g_s, t_own, t_in, lsem, ssem, rsem, ready,
):
    tile = lax.axis_index("space")
    me = lax.axis_index("bins")
    core = me % 2
    left, right = (tile + TILES - 1) % TILES, (tile + 1) % TILES
    mate = me + 1 - 2 * core

    def along(step):
        return (tile, (me + 2 * ZC + 2 * step) % (2 * ZC))

    barrier = pltpu.get_barrier_semaphore()
    partners = [(left, me), (right, me), (left, mate), (right, mate), (tile, mate), along(1), along(-1)]
    for who in partners:
        pl.semaphore_signal(barrier, inc=1, device_id=who, device_id_type=MESH)

    loads = [
        pltpu.make_async_copy(src, dst, lsem.at[n])
        for n, (src, dst) in enumerate(
            (
                (x_in, x_ref), (opt_in, opt_ref), (oval_in, oval_ref), (ovar_in, ovar_ref), (nb_in, nb_ref),
                (angle_in, angle_ref), (opw_in, opw_ref), (oty_in, oty_ref), (olist_in, olist_ref), (ocnt_in, ocnt_ref),
            )
        )
    ]
    for c in loads:
        c.start()

    def copy(src, dst, n, who):
        return pltpu.make_async_remote_copy(
            src_ref=src, dst_ref=dst, send_sem=ssem.at[n], recv_sem=rsem.at[n], device_id=who, device_id_type=MESH
        )

    lane = iota((MEM, 128), 1)
    block = lane // 32

    for c in loads[1:]:
        c.wait()
    zeros = jnp.zeros((1, OBS), F32)
    point = opt_ref[...]
    rows = [
        (point // ROWS).astype(F32), (point % ROWS).astype(F32), oval_ref[...], lax.rsqrt(ovar_ref[...]),
        zeros, zeros, zeros, zeros,
    ]
    packed = jnp.concatenate(rows, axis=0)
    meta[...] = jnp.concatenate([packed, jnp.zeros((8, OBS), F32)], axis=1)

    freq = (jnp.where(iota((BINS, PTS), 0) >= ND, 1, 0) + 2 * me).astype(F32)
    speed = COURANT_MAX * jnp.exp(-freq * math.log(FREQ_RATIO))
    open_side = (nb_ref[...] >= 0).astype(F32)
    cosine = jnp.concatenate([angle_ref[0]] * 2, axis=1)
    sine = jnp.concatenate([angle_ref[1]] * 2, axis=1)
    cx, cy = speed * jnp.abs(cosine), speed * jnp.abs(sine)
    a1[...] = 1.0 - cx - cy
    a2[...] = cx * jnp.where(cosine > 0, open_side[0:1], open_side[1:2])
    a3[...] = cy * jnp.where(sine > 0, open_side[2:3], open_side[3:4])

    here = (iota((PTS, OBS), 0) == point - tile * PTS).astype(BF16)
    kinds = (iota((16, OBS), 0) == oty_ref[...]).astype(F32)
    weights = lax.dot_general(
        opw_ref[...], kinds, (((0,), (0,)), ((), ())), precision=lax.Precision.HIGHEST, preferred_element_type=F32
    )

    at_obs = dot(jnp.concatenate([open_side, jnp.zeros((4, PTS), F32)], axis=0).astype(BF16), here)
    obs_col, obs_row = point // ROWS - tile * (PTS // ROWS), point % ROWS
    first_col = jnp.where(obs_col == 0, at_obs[0:1], 0.0)
    last_col = jnp.where(obs_col == PTS // ROWS - 1, at_obs[1:2], 0.0)
    in_row = (iota((ROWS, OBS), 0) == obs_row).astype(F32)
    carried = weights * cx[:, :OBS]
    for j in range(SIX):
        for bins, buf, on in ((WEST, edge_w, first_col), (EAST, edge_e, last_col)):
            rows4 = [in_row * (carried[f * ND + q * SIX + j : f * ND + q * SIX + j + 1] * on) for f, q in bins]
            buf[j] = jnp.concatenate(rows4, axis=0).astype(BF16)

    def pack(j):
        for bins, buf, half, at in ((WEST, send_w, 1, 96), (EAST, send_e, 0, 0)):
            out = None
            for k, (f, q) in enumerate(bins):
                edge = x_ref[f * ND + q * SIX + j, :, 128 * half : 128 * half + 128].astype(F32)
                edge = lanes_roll(edge, 32 * k - at)
                out = edge if out is None else jnp.where(block == k, edge, out)
            buf[j] = out.astype(BF16)

    loads[0].wait()
    for j in range(SIX):
        pack(j)

    pl.semaphore_wait(barrier, len(partners))
    halo = [
        copy(send_w, recv_w, 0, (right, me)),
        copy(send_e, recv_e, 1, (left, me)),
        copy(meta, meta_l, 2, (right, me)),
        copy(meta, meta_r, 3, (left, me)),
    ]
    halo[0].start()
    halo[1].start()
    for step in (1, -1):
        pl.semaphore_signal(ready.at[0], inc=1, device_id=along(step), device_id_type=MESH)
    halo[2].start()
    halo[3].start()

    def upwind(j, f, q, part):
        b = f * ND + q * SIX + j
        west = (f, q) in WEST
        mine = int(west == (part == 0))
        halves = [x_ref[b, :, 128 * h : 128 * h + 128].astype(F32) for h in range(2)]
        here_x = halves[mine]
        if part == 2:
            spot = (WEST if west else EAST).index((f, q))
            edge = (recv_w if west else recv_e)[j].astype(F32)
            edge = lanes_roll(edge, (0 if west else 96) - 32 * spot)
        else:
            edge = jnp.zeros((MEM, 128), F32)
        if west:
            other = lanes_roll(halves[0], 32) if part == 0 else edge
            inflow = jnp.where(block == 0, other, lanes_roll(here_x, 32))
        else:
            other = lanes_roll(halves[1], 96) if part == 0 else edge
            inflow = jnp.where(block == 3, other, lanes_roll(here_x, 96))
        beside_y = lanes_roll(here_x, 1 if q < 2 else 127)
        cut = slice(128 * mine, 128 * mine + 128)
        r1, r2, r3 = a1[b : b + 1, cut], a2[b : b + 1, cut], a3[b : b + 1, cut]
        fore[b, :, cut] = (here_x * r1 + inflow * r2 + beside_y * r3).astype(BF16)

    def upwind_all(*parts):
        for j in range(SIX):
            for f in range(2):
                for q in range(4):
                    for part in parts:
                        upwind(j, f, q, part)

    upwind_all(0, 1)

    predicted = jnp.zeros((MEM, OBS), F32)
    for part in range(4):
        at = dot(fore[12 * part : 12 * part + 12].reshape(12 * MEM, PTS), here)
        for i in range(12):
            b = 12 * part + i
            predicted += at[MEM * i : MEM * (i + 1)] * weights[b : b + 1]

    pl.semaphore_wait(ready.at[0], 2)
    for step in (2, -2):
        pl.semaphore_signal(ready.at[1], inc=1, device_id=along(step), device_id_type=MESH)

    ids = jnp.where(iota((MEM, PTS), 0) < ocnt_ref[...], olist_ref[...] - (tile - 1) * OBS, -1)
    ids = jnp.where(olist_ref[...] >= 0, ids, -1)
    low, high = ids[:, :128], ids[:, 128:]
    low = jnp.where(core == 0, low, lanes_roll(low, -32))
    high = jnp.where(core == 0, high, lanes_roll(high, -32))
    ids = jnp.where(
        block == 0, low, jnp.where(block == 1, lanes_roll(low, -32), jnp.where(block == 2, lanes_roll(high, 64), lanes_roll(high, 32)))
    )
    number = iota((NEAR, 128), 0)
    used = jnp.zeros((NEAR, 128), F32)
    for slot in range(MEM):
        used = jnp.where(ids[slot : slot + 1] == number, 1.0, used)

    halo[0].wait_recv()
    halo[1].wait_recv()
    for j in range(SIX):
        predicted += dot(recv_w[j], edge_w[j]) + dot(recv_e[j], edge_e[j])
    sums[...] = jnp.concatenate([predicted[:16], predicted[16:]], axis=1)
    pl.semaphore_wait(ready.at[1], 2)
    chip = me // 2
    far = []
    for n in range(ZC - 1):
        away = (n + (n + ZC - chip) // ZC + ZC - chip) % ZC
        far.append(copy(sums, z_in.at[away - 1], 4 + away, along(away)))
    for c in far:
        c.start()
    halo[2].wait_recv()
    halo[3].wait_recv()

    metas = jnp.concatenate(
        [
            jnp.where(iota((8, 128), 1) < OBS, meta_l[...], lanes_roll(meta[...], 64)),
            jnp.where(iota((8, 128), 1) < OBS, meta_r[...], 0.0),
        ],
        axis=1,
    )
    places = jnp.concatenate([metas, jnp.zeros((120, PTS), F32)], axis=0).T
    own_lane = iota((NEAR, 128), 1)
    col = (tile * 8 + 2 * (own_lane // 32) + core).astype(F32)
    row = (own_lane % 32).astype(F32)
    distance = (places[:NEAR, 0:1] - col) ** 2 + (places[:NEAR, 1:2] - row) ** 2
    taper = (1.0 - distance / (2.0 * LOC_R * LOC_R)) ** 2 * used
    taper_high, taper_low = split(taper)

    big_lane = iota((128, PTS), 1)
    target = 32 * ((big_lane // 32) % 4) + big_lane // 128
    source = iota((128, PTS), 0)
    for g in range(OWN):
        spread = (source == target + 2 * g).astype(BF16)
        expand[g] = spread
        w8[g] = dot(taper_high, spread).astype(BF16)

    upwind_all(2)

    def turn_in(i):
        f0, f1 = fore[2 * i].astype(F32), fore[2 * i + 1].astype(F32)
        parts = []
        for q in range(4):
            h = q // 2
            c0, c1 = f0[:, 128 * h : 128 * h + 128], f1[:, 128 * h : 128 * h + 128]
            if q % 2 == 0:
                parts.append(jnp.where(lane < 64, c0, lanes_roll(c1, 64)))
            else:
                parts.append(jnp.where(lane < 64, lanes_roll(c0, 64), c1))
        turned = jnp.concatenate(parts, axis=0).T
        relay[pl.ds(2 * i, 64, stride=BINS), :] = turned[:64]
        relay[pl.ds(2 * i + 1, 64, stride=BINS), :] = turned[64:]

    for i in range(BINS // 2):
        turn_in(i)

    for t in range(2 * GROUPS):
        operand[t] = relay[t * BINS : (t + 1) * BINS, :].astype(BF16)

    for c in far:
        c.wait_recv()
    acc = sums[...]
    for k in range(7):
        acc += z_in[k]
    total[...] = acc
    beside = [
        copy(total, total_l.at[0], 12, (right, me)),
        copy(total, total_r.at[0], 13, (left, me)),
        copy(total, total_l.at[1], 14, (right, mate)),
        copy(total, total_r.at[1], 15, (left, mate)),
        copy(total, total_m, 16, (tile, mate)),
    ]
    for c in beside:
        c.start()
    for c in beside:
        c.wait_recv()

    half = iota((16, 128), 1) < OBS
    pl_, po, pr = total_l[0] + total_l[1], total[...] + total_m[...], total_r[0] + total_r[1]
    first = jnp.where(half, pl_, lanes_roll(po, 64)), jnp.where(half, pr, 0.0)
    second = jnp.where(half, lanes_roll(pl_, 64), po), jnp.where(half, lanes_roll(pr, 64), 0.0)
    seen = jnp.concatenate([jnp.concatenate(first, axis=1), jnp.concatenate(second, axis=1)], axis=0)
    mean = jnp.sum(seen, axis=0, keepdims=True) * (1.0 / MEM)
    anomaly = (seen - mean) * metas[3:4]
    innovation = (metas[2:3] - mean) * metas[3:4]
    pulled = (anomaly * innovation)[:, :NEAR] * (1.0 / (MEM - 1))
    pull = folded(dot(stacked(pulled), taper_high)) + dot(pulled.astype(BF16), taper_low)
    pulls = stacked(pull)
    y_t = jnp.concatenate([anomaly] * 4, axis=0).T[:NEAR]
    y_t = jnp.concatenate([y_t, y_t], axis=1).astype(BF16)
    y = anomaly[:, :NEAR].astype(BF16)

    eye = (iota((MEM, PTS), 0) == iota((MEM, PTS), 1) % MEM).astype(F32)
    same = (iota((PTS, PTS), 0) // MEM == iota((PTS, PTS), 1) // MEM).astype(BF16)
    squares = []
    for g in range(OWN):
        matrix = eye + dot(y, w8[g] * y_t) * (1.0 / (MEM - 1))
        m_s[g] = matrix
        squares.append(jnp.sum(matrix * matrix, axis=0, keepdims=True))
        g_s[g] = folded(dot(pulls, expand[g]))
    norm = folded(dot(stacked(jnp.concatenate(squares, axis=0)), same))
    inv_scale = lax.rsqrt(norm)
    root_scale = jnp.sqrt(inv_scale)

    same_half = same[:128, :128]

    def newton(groups):
        for it in range(NS_ITERS):
            for g in groups:
                for h in range(2):
                    cut = slice(128 * h, 128 * h + 128)
                    current = m_s[g, :, cut]
                    if it == 0:
                        current = current * inv_scale[g : g + 1, cut]
                    step = 0.5 * (eye[:, cut] - current)
                    weight = block_diagonal(step, same_half)
                    if it == 0:
                        moved = current + dot(current.astype(BF16), weight)
                        z_s[g, :, cut] = eye[:, cut] + step
                    elif it == NS_ITERS - 1:
                        inverse = z_s[g, :, cut]
                        z_s[g, :, cut] = inverse + dot(inverse.astype(BF16), weight)
                        continue
                    else:
                        inverse = z_s[g, :, cut]
                        both = dot(jnp.concatenate([current, inverse], axis=0).astype(BF16), weight)
                        moved = current + both[:MEM]
                        z_s[g, :, cut] = inverse + both[MEM:]
                    m_s[g, :, cut] = moved + dot(moved.astype(BF16), weight)

    def mix(g):
        root = z_s[g] * root_scale[g : g + 1]
        half_step = jnp.sum(root * g_s[g], axis=0, keepdims=True)
        shift = folded(dot(stacked(root * half_step), same))
        mixed = root + shift
        mixed = mixed + (1.0 - jnp.sum(mixed, axis=0, keepdims=True)) * (1.0 / MEM)
        t_own[g] = mixed.astype(BF16)

    swaps = []
    for groups in BATCHES:
        newton(groups)
        for g in groups:
            mix(g)
            if g + 1 in SENT:
                first = SENT[SENT.index(g + 1) - 1]
                part = pl.ds(first, g + 1 - first)
                swap = copy(t_own.at[part], t_in.at[part], 17 + len(swaps), (tile, mate))
                swap.start()
                swaps.append(swap)

    def apply(owner, g, transform):
        for h in range(2):
            t = 2 * OWN * owner + 2 * g + h
            weight = block_diagonal(transform[g, :, 128 * h : 128 * h + 128], same_half)
            mixed_ref[pl.ds(t, BINS, stride=2 * GROUPS), :] = dot(operand[t], weight)

    for g in range(OWN):
        apply(core, g, t_own)
    for n, c in enumerate(swaps):
        c.wait_recv()
        for g in range(SENT[n], SENT[n + 1]):
            apply(1 - core, g, t_in)
    for c in halo + far + beside + swaps:
        c.wait_send()


def place_kernel(mixed_ref, out_hbm, out_ref, sem):
    lane = iota((MEM, 128), 1)
    copies = []
    for i in range(BINS // 2):
        turned = mixed_ref[128 * i : 128 * i + 128, :].T
        q = [turned[MEM * k : MEM * (k + 1)] for k in range(4)]
        for h in range(2):
            a, b = q[2 * h], q[2 * h + 1]
            cut = slice(128 * h, 128 * h + 128)
            out_ref[2 * i, :, cut] = jnp.where(lane < 64, a, lanes_roll(b, 64)).astype(BF16)
            out_ref[2 * i + 1, :, cut] = jnp.where(lane < 64, lanes_roll(a, 64), b).astype(BF16)
        if i % 4 == 3:
            part = pl.ds(2 * i - 6, 8)
            c = pltpu.make_async_copy(out_ref.at[part], out_hbm.at[part], sem.at[i // 4])
            c.start()
            copies.append(c)
    for c in copies:
        c.wait()


def per_device(x, neighbors, obs_operator, obs_point, obs_type, obs_value, obs_var, obs_list, obs_count):
    theta = 2.0 * np.pi * (np.arange(BINS) % ND + 0.5) / ND
    angles = np.stack([np.cos(theta), np.sin(theta)])[:, :, None]
    angles = jnp.asarray(np.broadcast_to(angles, (2, BINS, 128)), F32)
    vmem = pl.BlockSpec(memory_space=pltpu.VMEM)
    tile_f32 = pltpu.VMEM((16, 128), F32)
    operands = (
        angles, x, neighbors, obs_operator, obs_point[None], obs_type[None], obs_value[None], obs_var[None],
        obs_list, obs_count[None],
    )
    operands = [pltpu.with_memory_space_constraint(a, pltpu.HBM) for a in operands]
    mixed = pl.pallas_call(
        exchange_kernel,
        out_shape=jax.ShapeDtypeStruct((2 * GROUPS * BINS, 128), F32),
        in_specs=[pl.BlockSpec(memory_space=pltpu.HBM)] * 10,
        out_specs=vmem,
        scratch_shapes=[
            pltpu.VMEM((2, BINS, 128), F32),
            pltpu.VMEM((BINS, MEM, PTS), BF16),
            pltpu.VMEM((4, PTS), jnp.int32),
            pltpu.VMEM((16, BINS), F32),
            pltpu.VMEM((1, OBS), jnp.int32),
            pltpu.VMEM((1, OBS), jnp.int32),
            pltpu.VMEM((1, OBS), F32),
            pltpu.VMEM((1, OBS), F32),
            pltpu.VMEM((MEM, PTS), jnp.int32),
            pltpu.VMEM((1, PTS), jnp.int32),
            pltpu.VMEM((BINS, PTS), F32),
            pltpu.VMEM((BINS, PTS), F32),
            pltpu.VMEM((BINS, PTS), F32),
            pltpu.VMEM((SIX, MEM, 128), BF16),
            pltpu.VMEM((SIX, MEM, 128), BF16),
            pltpu.VMEM((SIX, MEM, 128), BF16),
            pltpu.VMEM((SIX, MEM, 128), BF16),
            pltpu.VMEM((SIX, 128, OBS), BF16),
            pltpu.VMEM((SIX, 128, OBS), BF16),
            pltpu.VMEM((8, 128), F32),
            pltpu.VMEM((8, 128), F32),
            pltpu.VMEM((8, 128), F32),
            pltpu.VMEM((BINS, MEM, PTS), BF16),
            tile_f32,
            pltpu.VMEM((7, 16, 128), F32),
            tile_f32,
            tile_f32,
            pltpu.VMEM((2, 16, 128), F32),
            pltpu.VMEM((2, 16, 128), F32),
            pltpu.VMEM((64 * BINS, 128), F32),
            pltpu.VMEM((2 * GROUPS, BINS, 128), BF16),
            pltpu.VMEM((OWN, NEAR, PTS), BF16),
            pltpu.VMEM((OWN, 128, PTS), BF16),
            pltpu.VMEM((OWN, MEM, PTS), F32),
            pltpu.VMEM((OWN, MEM, PTS), F32),
            pltpu.VMEM((OWN, MEM, PTS), F32),
            pltpu.VMEM((OWN, MEM, PTS), BF16),
            pltpu.VMEM((OWN, MEM, PTS), BF16),
            pltpu.SemaphoreType.DMA((10,)),
            pltpu.SemaphoreType.DMA((20,)),
            pltpu.SemaphoreType.DMA((20,)),
            pltpu.SemaphoreType.REGULAR((2,)),
        ],
        compiler_params=pltpu.CompilerParams(
            collective_id=0, has_side_effects=True, vmem_limit_bytes=40 << 20
        ),
        name="exchange",
    )(*operands)
    return pl.pallas_call(
        place_kernel,
        out_shape=jax.ShapeDtypeStruct((BINS, MEM, PTS), BF16),
        in_specs=[vmem],
        out_specs=pl.BlockSpec(memory_space=pl.ANY),
        scratch_shapes=[pltpu.VMEM((BINS, MEM, PTS), BF16), pltpu.SemaphoreType.DMA((SIX,))],
        compiler_params=pltpu.CompilerParams(vmem_limit_bytes=40 << 20),
        name="place",
    )(mixed)


def solution(mesh):
    placed = (
        P("bins", None, "space"),
        P(None, "space"),
        P(None, "bins"),
        P("space"),
        P("space"),
        P("space"),
        P("space"),
        P(None, "space"),
        P("space"),
    )
    return jax.shard_map(
        per_device, mesh=mesh, in_specs=placed, out_specs=P("bins", None, "space"), check_vma=False
    )
```

```python
import functools
import math

import jax
import jax.numpy as jnp
import numpy as np
from jax import lax
from jax.experimental import pallas as pl
from jax.experimental.pallas import tpu as pltpu
from jax.sharding import PartitionSpec as P

ND = 24
ROWS = 32
LOC_R = 6
NS_ITERS = 8
COURANT_MAX = 0.7
FREQ_RATIO = 1.1

BINS = 48
MEM = 32
PTS = 256
OBS = 64
NEAR = 3 * OBS
OWN = 16
GROUPS = 2 * OWN
TILES = 32
ZC = 8
BATCHES = (range(8), range(8, 16))
SENT = (0, 8, 12, 16)
SIX = 6
WEST = ((0, 0), (0, 3), (1, 0), (1, 3))
EAST = ((0, 1), (0, 2), (1, 1), (1, 2))

MESH = pl.DeviceIdType.MESH
F32 = jnp.float32
BF16 = jnp.bfloat16


def iota(shape, dim):
    return lax.broadcasted_iota(jnp.int32, shape, dim)


def dot(a, b):
    return jnp.dot(a, b, preferred_element_type=F32)


def split(a):
    high = a.astype(BF16)
    return high, (a - high.astype(F32)).astype(BF16)


def stacked(a):
    return jnp.concatenate(split(a), axis=0)


def folded(a):
    half = a.shape[0] // 2
    return a[:half] + a[half:]


def block_diagonal(rows, mask):
    return jnp.concatenate([rows.astype(BF16)] * (mask.shape[0] // MEM), axis=0) * mask


def lanes_roll(a, by):
    return pltpu.roll(a, by % 128, 1)


def exchange_kernel(
    angle_in, x_in, nb_in, opw_in, opt_in, oty_in, oval_in, ovar_in, olist_in, ocnt_in,
    mixed_ref,
    angle_ref, x_ref, nb_ref, opw_ref, opt_ref, oty_ref, oval_ref, ovar_ref, olist_ref, ocnt_ref,
    a1, a2, a3, send_w, send_e, recv_w, recv_e, edge_w, edge_e, meta, meta_l, meta_r, fore, sums, z_in, total, total_m,
    total_l, total_r, relay, operand, w8, expand, m_s, z_s, g_s, t_own, t_in, lsem, ssem, rsem, ready,
):
    tile = lax.axis_index("space")
    me = lax.axis_index("bins")
    core = me % 2
    left, right = (tile + TILES - 1) % TILES, (tile + 1) % TILES
    mate = me + 1 - 2 * core

    def along(step):
        return (tile, (me + 2 * ZC + 2 * step) % (2 * ZC))

    barrier = pltpu.get_barrier_semaphore()
    partners = [(left, me), (right, me), (left, mate), (right, mate), (tile, mate), along(1), along(-1)]
    for who in partners:
        pl.semaphore_signal(barrier, inc=1, device_id=who, device_id_type=MESH)

    loads = [
        pltpu.make_async_copy(src, dst, lsem.at[n])
        for n, (src, dst) in enumerate(
            (
                (x_in, x_ref), (opt_in, opt_ref), (oval_in, oval_ref), (ovar_in, ovar_ref), (nb_in, nb_ref),
                (angle_in, angle_ref), (opw_in, opw_ref), (oty_in, oty_ref), (olist_in, olist_ref), (ocnt_in, ocnt_ref),
            )
        )
    ]
    for c in loads:
        c.start()

    def copy(src, dst, n, who):
        return pltpu.make_async_remote_copy(
            src_ref=src, dst_ref=dst, send_sem=ssem.at[n], recv_sem=rsem.at[n], device_id=who, device_id_type=MESH
        )

    lane = iota((MEM, 128), 1)
    block = lane // 32

    for c in loads[1:]:
        c.wait()
    zeros = jnp.zeros((1, OBS), F32)
    point = opt_ref[...]
    rows = [
        (point // ROWS).astype(F32), (point % ROWS).astype(F32), oval_ref[...], lax.rsqrt(ovar_ref[...]),
        zeros, zeros, zeros, zeros,
    ]
    packed = jnp.concatenate(rows, axis=0)
    meta[...] = jnp.concatenate([packed, jnp.zeros((8, OBS), F32)], axis=1)

    freq = (jnp.where(iota((BINS, PTS), 0) >= ND, 1, 0) + 2 * me).astype(F32)
    speed = COURANT_MAX * jnp.exp(-freq * math.log(FREQ_RATIO))
    open_side = (nb_ref[...] >= 0).astype(F32)
    cosine = jnp.concatenate([angle_ref[0]] * 2, axis=1)
    sine = jnp.concatenate([angle_ref[1]] * 2, axis=1)
    cx, cy = speed * jnp.abs(cosine), speed * jnp.abs(sine)
    a1[...] = 1.0 - cx - cy
    a2[...] = cx * jnp.where(cosine > 0, open_side[0:1], open_side[1:2])
    a3[...] = cy * jnp.where(sine > 0, open_side[2:3], open_side[3:4])

    here = (iota((PTS, OBS), 0) == point - tile * PTS).astype(BF16)
    kinds = (iota((16, OBS), 0) == oty_ref[...]).astype(F32)
    weights = lax.dot_general(
        opw_ref[...], kinds, (((0,), (0,)), ((), ())), precision=lax.Precision.HIGHEST, preferred_element_type=F32
    )

    at_obs = dot(jnp.concatenate([open_side, jnp.zeros((4, PTS), F32)], axis=0).astype(BF16), here)
    obs_col, obs_row = point // ROWS - tile * (PTS // ROWS), point % ROWS
    first_col = jnp.where(obs_col == 0, at_obs[0:1], 0.0)
    last_col = jnp.where(obs_col == PTS // ROWS - 1, at_obs[1:2], 0.0)
    in_row = (iota((ROWS, OBS), 0) == obs_row).astype(F32)
    carried = weights * cx[:, :OBS]
    for j in range(SIX):
        for bins, buf, on in ((WEST, edge_w, first_col), (EAST, edge_e, last_col)):
            rows4 = [in_row * (carried[f * ND + q * SIX + j : f * ND + q * SIX + j + 1] * on) for f, q in bins]
            buf[128 * j : 128 * j + 128, :] = jnp.concatenate(rows4, axis=0).astype(BF16)

    def pack(j):
        for bins, buf, half, at in ((WEST, send_w, 1, 96), (EAST, send_e, 0, 0)):
            out = None
            for k, (f, q) in enumerate(bins):
                edge = x_ref[f * ND + q * SIX + j, :, 128 * half : 128 * half + 128].astype(F32)
                edge = lanes_roll(edge, 32 * k - at)
                out = edge if out is None else jnp.where(block == k, edge, out)
            buf[j] = out.astype(BF16)

    loads[0].wait()
    for j in range(SIX):
        pack(j)

    pl.semaphore_wait(barrier, len(partners))
    halo = [
        copy(send_w, recv_w, 0, (right, me)),
        copy(send_e, recv_e, 1, (left, me)),
        copy(meta, meta_l, 2, (right, me)),
        copy(meta, meta_r, 3, (left, me)),
    ]
    halo[0].start()
    halo[1].start()
    for step in (1, -1):
        pl.semaphore_signal(ready.at[0], inc=1, device_id=along(step), device_id_type=MESH)
    halo[2].start()
    halo[3].start()

    def upwind(j, f, q, part):
        b = f * ND + q * SIX + j
        west = (f, q) in WEST
        mine = int(west == (part == 0))
        halves = [x_ref[b, :, 128 * h : 128 * h + 128].astype(F32) for h in range(2)]
        here_x = halves[mine]
        if part == 2:
            spot = (WEST if west else EAST).index((f, q))
            edge = (recv_w if west else recv_e)[j].astype(F32)
            edge = lanes_roll(edge, (0 if west else 96) - 32 * spot)
        else:
            edge = jnp.zeros((MEM, 128), F32)
        if west:
            other = lanes_roll(halves[0], 32) if part == 0 else edge
            inflow = jnp.where(block == 0, other, lanes_roll(here_x, 32))
        else:
            other = lanes_roll(halves[1], 96) if part == 0 else edge
            inflow = jnp.where(block == 3, other, lanes_roll(here_x, 96))
        beside_y = lanes_roll(here_x, 1 if q < 2 else 127)
        cut = slice(128 * mine, 128 * mine + 128)
        r1, r2, r3 = a1[b : b + 1, cut], a2[b : b + 1, cut], a3[b : b + 1, cut]
        fore[b, :, cut] = (here_x * r1 + inflow * r2 + beside_y * r3).astype(BF16)

    def upwind_all(*parts):
        for j in range(SIX):
            for f in range(2):
                for q in range(4):
                    for part in parts:
                        upwind(j, f, q, part)

    upwind_all(0, 1)

    predicted = jnp.zeros((MEM, OBS), F32)
    for part in range(4):
        at = dot(fore[12 * part : 12 * part + 12].reshape(12 * MEM, PTS), here)
        for i in range(12):
            b = 12 * part + i
            predicted += at[MEM * i : MEM * (i + 1)] * weights[b : b + 1]

    pl.semaphore_wait(ready.at[0], 2)
    for step in (2, -2):
        pl.semaphore_signal(ready.at[1], inc=1, device_id=along(step), device_id_type=MESH)

    ids = jnp.where(iota((MEM, PTS), 0) < ocnt_ref[...], olist_ref[...] - (tile - 1) * OBS, -1)
    ids = jnp.where(olist_ref[...] >= 0, ids, -1)
    low, high = ids[:, :128], ids[:, 128:]
    low = jnp.where(core == 0, low, lanes_roll(low, -32))
    high = jnp.where(core == 0, high, lanes_roll(high, -32))
    ids = jnp.where(
        block == 0, low, jnp.where(block == 1, lanes_roll(low, -32), jnp.where(block == 2, lanes_roll(high, 64), lanes_roll(high, 32)))
    )
    number = iota((NEAR, 128), 0)
    used = jnp.zeros((NEAR, 128), F32)
    for slot in range(MEM):
        used = jnp.where(ids[slot : slot + 1] == number, 1.0, used)

    halo[0].wait_recv()
    halo[1].wait_recv()
    for buf, weight in ((recv_w, edge_w), (recv_e, edge_e)):
        predicted += dot(jnp.concatenate([buf[j] for j in range(SIX)], axis=1), weight[...])
    sums[...] = jnp.concatenate([predicted[:16], predicted[16:]], axis=1)
    pl.semaphore_wait(ready.at[1], 2)
    chip = me // 2
    far = []
    for n in range(ZC - 1):
        away = (n + (n + ZC - chip) // ZC + ZC - chip) % ZC
        far.append(copy(sums, z_in.at[away - 1], 4 + away, along(away)))
    for c in far:
        c.start()
    halo[2].wait_recv()
    halo[3].wait_recv()

    metas = jnp.concatenate(
        [
            jnp.where(iota((8, 128), 1) < OBS, meta_l[...], lanes_roll(meta[...], 64)),
            jnp.where(iota((8, 128), 1) < OBS, meta_r[...], 0.0),
        ],
        axis=1,
    )
    places = jnp.concatenate([metas, jnp.zeros((120, PTS), F32)], axis=0).T
    own_lane = iota((NEAR, 128), 1)
    col = (tile * 8 + 2 * (own_lane // 32) + core).astype(F32)
    row = (own_lane % 32).astype(F32)
    distance = (places[:NEAR, 0:1] - col) ** 2 + (places[:NEAR, 1:2] - row) ** 2
    taper = (1.0 - distance / (2.0 * LOC_R * LOC_R)) ** 2 * used
    taper_high, taper_low = split(taper)

    big_lane = iota((128, PTS), 1)
    target = 32 * ((big_lane // 32) % 4) + big_lane // 128
    source = iota((128, PTS), 0)
    for g in range(OWN):
        spread = (source == target + 2 * g).astype(BF16)
        expand[g] = spread
        w8[g] = dot(taper_high, spread).astype(BF16)

    upwind_all(2)

    def turn_in(i):
        f0, f1 = fore[2 * i].astype(F32), fore[2 * i + 1].astype(F32)
        parts = []
        for q in range(4):
            h = q // 2
            c0, c1 = f0[:, 128 * h : 128 * h + 128], f1[:, 128 * h : 128 * h + 128]
            if q % 2 == 0:
                parts.append(jnp.where(lane < 64, c0, lanes_roll(c1, 64)))
            else:
                parts.append(jnp.where(lane < 64, lanes_roll(c0, 64), c1))
        turned = jnp.concatenate(parts, axis=0).T
        relay[pl.ds(2 * i, 64, stride=BINS), :] = turned[:64]
        relay[pl.ds(2 * i + 1, 64, stride=BINS), :] = turned[64:]

    for i in range(BINS // 2):
        turn_in(i)

    for t in range(2 * GROUPS):
        operand[t] = relay[t * BINS : (t + 1) * BINS, :].astype(BF16)

    for c in far:
        c.wait_recv()
    acc = sums[...]
    for k in range(7):
        acc += z_in[k]
    total[...] = acc
    beside = [
        copy(total, total_l.at[0], 12, (right, me)),
        copy(total, total_r.at[0], 13, (left, me)),
        copy(total, total_l.at[1], 14, (right, mate)),
        copy(total, total_r.at[1], 15, (left, mate)),
        copy(total, total_m, 16, (tile, mate)),
    ]
    for c in beside:
        c.start()
    for c in beside:
        c.wait_recv()

    half = iota((16, 128), 1) < OBS
    pl_, po, pr = total_l[0] + total_l[1], total[...] + total_m[...], total_r[0] + total_r[1]
    first = jnp.where(half, pl_, lanes_roll(po, 64)), jnp.where(half, pr, 0.0)
    second = jnp.where(half, lanes_roll(pl_, 64), po), jnp.where(half, lanes_roll(pr, 64), 0.0)
    seen = jnp.concatenate([jnp.concatenate(first, axis=1), jnp.concatenate(second, axis=1)], axis=0)
    mean = jnp.sum(seen, axis=0, keepdims=True) * (1.0 / MEM)
    anomaly = (seen - mean) * metas[3:4]
    innovation = (metas[2:3] - mean) * metas[3:4]
    pulled = (anomaly * innovation)[:, :NEAR] * (1.0 / (MEM - 1))
    pull = folded(dot(stacked(pulled), taper_high)) + dot(pulled.astype(BF16), taper_low)
    pulls = stacked(pull)
    y_t = jnp.concatenate([anomaly] * 4, axis=0).T[:NEAR]
    y_t = jnp.concatenate([y_t, y_t], axis=1).astype(BF16)
    y = anomaly[:, :NEAR].astype(BF16)

    eye = (iota((MEM, PTS), 0) == iota((MEM, PTS), 1) % MEM).astype(F32)
    same = (iota((PTS, PTS), 0) // MEM == iota((PTS, PTS), 1) // MEM).astype(BF16)
    inv_scale, root_scale = {}, {}
    for groups in BATCHES:
        squares = []
        for g in groups:
            matrix = eye + dot(y, w8[g] * y_t) * (1.0 / (MEM - 1))
            m_s[g] = matrix
            squares.append(jnp.sum(matrix * matrix, axis=0, keepdims=True))
        norm = folded(dot(stacked(jnp.concatenate(squares, axis=0)), same))
        for n, g in enumerate(groups):
            inv_scale[g] = lax.rsqrt(norm[n : n + 1])
            root_scale[g] = jnp.sqrt(inv_scale[g])
    for g in range(OWN):
        g_s[g] = folded(dot(pulls, expand[g]))

    same_half = same[:128, :128]

    def newton(groups):
        for it in range(NS_ITERS):
            for g in groups:
                for h in range(2):
                    cut = slice(128 * h, 128 * h + 128)
                    current = m_s[g, :, cut]
                    if it == 0:
                        current = current * inv_scale[g][:, cut]
                    step = 0.5 * (eye[:, cut] - current)
                    weight = block_diagonal(step, same_half)
                    if it == 0:
                        moved = current + dot(current.astype(BF16), weight)
                        z_s[g, :, cut] = eye[:, cut] + step
                    elif it == NS_ITERS - 1:
                        inverse = z_s[g, :, cut]
                        z_s[g, :, cut] = inverse + dot(inverse.astype(BF16), weight)
                        continue
                    else:
                        inverse = z_s[g, :, cut]
                        both = dot(jnp.concatenate([current, inverse], axis=0).astype(BF16), weight)
                        moved = current + both[:MEM]
                        z_s[g, :, cut] = inverse + both[MEM:]
                    m_s[g, :, cut] = moved + dot(moved.astype(BF16), weight)

    def mix(g):
        root = z_s[g] * root_scale[g]
        half_step = jnp.sum(root * g_s[g], axis=0, keepdims=True)
        shift = folded(dot(stacked(root * half_step), same))
        mixed = root + shift
        mixed = mixed + (1.0 - jnp.sum(mixed, axis=0, keepdims=True)) * (1.0 / MEM)
        t_own[g] = mixed.astype(BF16)

    swaps = []
    for groups in BATCHES:
        newton(groups)
        for g in groups:
            mix(g)
            if g + 1 in SENT:
                first = SENT[SENT.index(g + 1) - 1]
                part = pl.ds(first, g + 1 - first)
                swap = copy(t_own.at[part], t_in.at[part], 17 + len(swaps), (tile, mate))
                swap.start()
                swaps.append(swap)

    def apply(owner, g, transform):
        for h in range(2):
            t = 2 * OWN * owner + 2 * g + h
            weight = block_diagonal(transform[g, :, 128 * h : 128 * h + 128], same_half)
            mixed_ref[pl.ds(t, BINS, stride=2 * GROUPS), :] = dot(operand[t], weight)

    for g in range(OWN):
        apply(core, g, t_own)
    for n, c in enumerate(swaps):
        c.wait_recv()
        for g in range(SENT[n], SENT[n + 1]):
            apply(1 - core, g, t_in)
    for c in halo + far + beside + swaps:
        c.wait_send()


def place_kernel(mixed_ref, out_hbm, out_ref, sem):
    lane = iota((MEM, 128), 1)
    copies = []
    for i in range(BINS // 2):
        turned = mixed_ref[128 * i : 128 * i + 128, :].T
        q = [turned[MEM * k : MEM * (k + 1)] for k in range(4)]
        for h in range(2):
            a, b = q[2 * h], q[2 * h + 1]
            cut = slice(128 * h, 128 * h + 128)
            out_ref[2 * i, :, cut] = jnp.where(lane < 64, a, lanes_roll(b, 64)).astype(BF16)
            out_ref[2 * i + 1, :, cut] = jnp.where(lane < 64, lanes_roll(a, 64), b).astype(BF16)
        if i % 4 == 3:
            part = pl.ds(2 * i - 6, 8)
            c = pltpu.make_async_copy(out_ref.at[part], out_hbm.at[part], sem.at[i // 4])
            c.start()
            copies.append(c)
    for c in copies:
        c.wait()


def per_device(x, neighbors, obs_operator, obs_point, obs_type, obs_value, obs_var, obs_list, obs_count):
    theta = 2.0 * np.pi * (np.arange(BINS) % ND + 0.5) / ND
    angles = np.stack([np.cos(theta), np.sin(theta)])[:, :, None]
    angles = jnp.asarray(np.broadcast_to(angles, (2, BINS, 128)), F32)
    vmem = pl.BlockSpec(memory_space=pltpu.VMEM)
    tile_f32 = pltpu.VMEM((16, 128), F32)
    operands = (
        angles, x, neighbors, obs_operator, obs_point[None], obs_type[None], obs_value[None], obs_var[None],
        obs_list, obs_count[None],
    )
    operands = [pltpu.with_memory_space_constraint(a, pltpu.HBM) for a in operands]
    mixed = pl.pallas_call(
        exchange_kernel,
        out_shape=jax.ShapeDtypeStruct((2 * GROUPS * BINS, 128), F32),
        in_specs=[pl.BlockSpec(memory_space=pltpu.HBM)] * 10,
        out_specs=vmem,
        scratch_shapes=[
            pltpu.VMEM((2, BINS, 128), F32),
            pltpu.VMEM((BINS, MEM, PTS), BF16),
            pltpu.VMEM((4, PTS), jnp.int32),
            pltpu.VMEM((16, BINS), F32),
            pltpu.VMEM((1, OBS), jnp.int32),
            pltpu.VMEM((1, OBS), jnp.int32),
            pltpu.VMEM((1, OBS), F32),
            pltpu.VMEM((1, OBS), F32),
            pltpu.VMEM((MEM, PTS), jnp.int32),
            pltpu.VMEM((1, PTS), jnp.int32),
            pltpu.VMEM((BINS, PTS), F32),
            pltpu.VMEM((BINS, PTS), F32),
            pltpu.VMEM((BINS, PTS), F32),
            pltpu.VMEM((SIX, MEM, 128), BF16),
            pltpu.VMEM((SIX, MEM, 128), BF16),
            pltpu.VMEM((SIX, MEM, 128), BF16),
            pltpu.VMEM((SIX, MEM, 128), BF16),
            pltpu.VMEM((SIX * 128, OBS), BF16),
            pltpu.VMEM((SIX * 128, OBS), BF16),
            pltpu.VMEM((8, 128), F32),
            pltpu.VMEM((8, 128), F32),
            pltpu.VMEM((8, 128), F32),
            pltpu.VMEM((BINS, MEM, PTS), BF16),
            tile_f32,
            pltpu.VMEM((7, 16, 128), F32),
            tile_f32,
            tile_f32,
            pltpu.VMEM((2, 16, 128), F32),
            pltpu.VMEM((2, 16, 128), F32),
            pltpu.VMEM((64 * BINS, 128), F32),
            pltpu.VMEM((2 * GROUPS, BINS, 128), BF16),
            pltpu.VMEM((OWN, NEAR, PTS), BF16),
            pltpu.VMEM((OWN, 128, PTS), BF16),
            pltpu.VMEM((OWN, MEM, PTS), F32),
            pltpu.VMEM((OWN, MEM, PTS), F32),
            pltpu.VMEM((OWN, MEM, PTS), F32),
            pltpu.VMEM((OWN, MEM, PTS), BF16),
            pltpu.VMEM((OWN, MEM, PTS), BF16),
            pltpu.SemaphoreType.DMA((10,)),
            pltpu.SemaphoreType.DMA((20,)),
            pltpu.SemaphoreType.DMA((20,)),
            pltpu.SemaphoreType.REGULAR((2,)),
        ],
        compiler_params=pltpu.CompilerParams(
            collective_id=0, has_side_effects=True, vmem_limit_bytes=40 << 20
        ),
        name="exchange",
    )(*operands)
    return pl.pallas_call(
        place_kernel,
        out_shape=jax.ShapeDtypeStruct((BINS, MEM, PTS), BF16),
        in_specs=[vmem],
        out_specs=pl.BlockSpec(memory_space=pl.ANY),
        scratch_shapes=[pltpu.VMEM((BINS, MEM, PTS), BF16), pltpu.SemaphoreType.DMA((SIX,))],
        compiler_params=pltpu.CompilerParams(vmem_limit_bytes=40 << 20),
        name="place",
    )(mixed)


def solution(mesh):
    placed = (
        P("bins", None, "space"),
        P(None, "space"),
        P(None, "bins"),
        P("space"),
        P("space"),
        P("space"),
        P("space"),
        P(None, "space"),
        P("space"),
    )
    return jax.shard_map(
        per_device, mesh=mesh, in_specs=placed, out_specs=P("bins", None, "space"), check_vma=False
    )
```
